128 devices in a mesh: region: 32 (over x, y, core), sub: 4 (over z).
Axes of the slice: x: 4, y: 4, z: 4, core: 2. Of those that a mesh axis runs over, the one named last changes fastest.
Arguments:
- interior_inverse: float32 [512, 512, 512], P(('region', 'sub')), may hold values from -0.12 to 12, as said below
- coupling: float32 [512, 4, 512, 128], P(('region', 'sub')), may hold values from -0.25 to 0.25
- interior_grad: float32 [512, 512, 128], P(('region', 'sub')), may hold values from -6 to 6
- separator_hessian_blocks: float32 [512, 128, 128], P(('region', 'sub')), may hold values from -12 to 290, as said below
- sep_grad: float32 [512, 128, 128], P(('region', 'sub')), may hold values from -384 to 384
- lists: int32 [512, 4], replicated, may hold values from 0 to 511, as said below
- owner: int32 [512], replicated, may hold values from 0 to 511, as said below
- counts: int32 [512], replicated, may hold values from 1 to 4
Outputs:
- interior_solution: float32 [512, 512, 128], P(('region', 'sub'))
- separator_solution: float32 [512, 128, 128], P(('region', 'sub'))
- separator_residual: float32 [512, 128, 128], P(('region', 'sub'))
The draws below stay inside these ranges and needn't reach their ends.
Inputs may be any that keep to these rules, and one draw needn't show every extreme that they name: `owner`: A permutation of the 512 positions; position p lies on device p // 4 in the order region, then sub. Submap i lies on device i // 4. Each submap lists distinct tiles. Every listing names a tile owned by a device of the submap's region or of the next region (the last region's next is the first); of the 16 listings of one device, exactly 2 name tiles of each of these 8 owners. Only the first counts[i] listings of submap i are live. `interior_inverse`: symmetric positive definite. `separator_hessian_blocks`: Symmetric; with the couplings the whole system is positive definite.
All inputs are finite; a program needn't handle non-finite values.
Results may differ from the reference program's by a relative error of at most 0.0003.
Values sent between devices are 32-bit elements; how exact they have to be, the bound alone decides.
No kernel may reach another device: no remote copies, remote signals or barrier semaphores. Data moves between devices by JAX's collectives and lax.ppermute only.
A program may use at most 128 MiB of HBM per device.

```python
import math
import jax
import jax.numpy as jnp
from jax import lax

NI = 512
TILE = 128
NRHS = 128
SLOTS = 4
CHEB = 2
SUB_DEV = 4
SEP_DEV = 4
SUBMAPS = 512
NSEP = 512
N_REGION = 32
N_SUB = 4


def owner_perm(key):
    return jax.random.permutation(jax.random.fold_in(key, 101), NSEP)


def draw_owner(key, part):
    return owner_perm(key).astype(jnp.int32)


def draw_lists(key, part):
    perm = owner_perm(key).astype(jnp.int32)
    key = jax.random.fold_in(key, 3)
    key_slots, key_local = jax.random.split(key)
    per_dev = SUB_DEV * SLOTS
    capacity = per_dev // (2 * N_SUB)
    devices = N_REGION * N_SUB
    slot_scores = jax.random.randint(key_slots, (devices, per_dev), 0, 1 << 16) * per_dev + jnp.arange(per_dev)[None, :]
    sigma = jnp.argsort(slot_scores, axis=1).astype(jnp.int32)
    dest = sigma // capacity
    rank = sigma % capacity
    local_scores = jax.random.randint(key_local, (devices, 2 * N_SUB, SEP_DEV), 0, 1 << 16) * SEP_DEV + jnp.arange(SEP_DEV)[None, None, :]
    local_perm = jnp.argsort(local_scores, axis=2).astype(jnp.int32)
    picked = jnp.take_along_axis(local_perm, dest[:, :, None], axis=1)
    resident_tile = jnp.take_along_axis(picked, rank[:, :, None], axis=2)[:, :, 0]
    device_ids = jnp.arange(devices)[:, None]
    region_ids = device_ids // N_SUB
    owner_dev = (region_ids + dest // N_SUB) % N_REGION * N_SUB + dest % N_SUB
    position = owner_dev * SEP_DEV + resident_tile
    inverse = jnp.argsort(perm).astype(jnp.int32)
    return inverse[position].reshape(SUBMAPS, SLOTS).astype(jnp.int32)


def draw_interior_inverse(key, part):
    key = jax.random.fold_in(key, 5)
    key_off, key_diag = jax.random.split(key, 2)
    limit = 1.8 / NI
    raw = jax.random.uniform(key_off, (SUBMAPS, NI, NI), jnp.float32, -limit, limit)
    sym = 0.5 * (raw + jnp.swapaxes(raw, 1, 2))
    eye_mat = jnp.eye(NI, dtype=jnp.float32)
    diag_vals = jax.random.uniform(key_diag, (SUBMAPS, NI), jnp.float32, 2.0, 3.0)
    matrix = sym * (1.0 - eye_mat) + eye_mat * diag_vals[:, :, None]
    return matrix.astype(jnp.float32)


def draw_separator_hessian_blocks(key, part):
    key = jax.random.fold_in(key, 9)
    key_off, key_level, key_rows, key_mean = jax.random.split(key, 4)
    raw = jax.random.uniform(key_off, (NSEP, TILE, TILE), jnp.float32, -0.054, 0.054)
    sym = 0.5 * (raw + jnp.swapaxes(raw, 1, 2))
    mean_part = jax.random.uniform(key_mean, (NSEP,), jnp.float32, 0.006, 0.0078)
    eye_mat = jnp.eye(TILE, dtype=jnp.float32)
    level = jnp.exp(jax.random.uniform(key_level, (NSEP,), jnp.float32, math.log(120.0), math.log(240.0)))
    rows = jax.random.uniform(key_rows, (NSEP, TILE), jnp.float32, 1.0, 1.2)
    offdiag = level[:, None, None] * (sym + mean_part[:, None, None])
    matrix = offdiag * (1.0 - eye_mat) + eye_mat * (level[:, None] * rows)[:, :, None]
    return matrix.astype(jnp.float32)


def touch_ends(drawn, own_key, smallest, top_value):
    longest = drawn.shape.index(max(drawn.shape))
    spots = []
    for shift in (0, 1):
        where = [jax.random.randint(jax.random.fold_in(own_key, axis), (), 0, length) for axis, length in enumerate(drawn.shape)]
        where[longest] = (where[longest] + shift) % drawn.shape[longest]
        spots.append(tuple(where))
    return drawn.at[spots[0]].set(smallest).at[spots[1]].set(top_value)


def block_scale(rng, dims, shards, low, high):
    def one(dim, blocks):
        steps = jax.random.uniform(jax.random.fold_in(jax.random.fold_in(rng, 6), dim), (blocks,), jnp.float32, low / len(shards), high / len(shards))
        return jnp.repeat(jnp.exp(steps), dims[dim] // blocks).reshape((-1,) + (1,) * (len(dims) - dim - 1))

    level = one(*shards[0])
    for cut in shards[1:]:
        level = level * one(*cut)
    return level


def scatter_about(own_key, dims, spread, bound, cuts=(), kind=jnp.bfloat16):
    level = block_scale(own_key, dims, cuts, -0.22, 0.18) if cuts else 1.0
    drawn = jax.random.normal(own_key, dims, jnp.float32) * spread * level
    return jnp.minimum(jnp.maximum(drawn, -bound), bound).astype(kind)


def setup_inputs(seed: int = 0) -> dict:
    key_list = jax.random.split(jax.random.key(seed), 9)
    interior_inverse = draw_interior_inverse(jax.random.fold_in(key_list[8], 71), 0)
    coupling = scatter_about(key_list[1], (SUBMAPS, SLOTS, NI, TILE), NI ** -0.5, 0.25, ((0, 128),), jnp.float32)
    interior_grad = scatter_about(key_list[2], (SUBMAPS, NI, NRHS), 1.0, 6.0, ((0, 128),), jnp.float32)
    separator_hessian_blocks = draw_separator_hessian_blocks(jax.random.fold_in(key_list[8], 71), 0)
    sep_grad = scatter_about(key_list[4], (NSEP, TILE, NRHS), 64.0, 384.0, ((0, 128),), jnp.float32)
    lists = draw_lists(jax.random.fold_in(key_list[8], 71), 0)
    owner = draw_owner(jax.random.fold_in(key_list[8], 71), 0)
    counts = touch_ends(jax.random.randint(key_list[7], (SUBMAPS,), 1, SLOTS + 1), jax.random.fold_in(key_list[7], 1), 1, SLOTS).astype(jnp.int32)
    return dict(interior_inverse=interior_inverse, coupling=coupling, interior_grad=interior_grad, separator_hessian_blocks=separator_hessian_blocks, sep_grad=sep_grad, lists=lists, owner=owner, counts=counts)


TOP_ACCURACY = lax.Precision.HIGHEST

def tile_solve(factor_tile, right_tile):
    return jax.scipy.linalg.cho_solve((factor_tile, True), right_tile)

def reference(interior_inverse, coupling, interior_grad, separator_hessian_blocks, sep_grad, lists, owner, counts):
    live_mask = (jnp.arange(SLOTS)[None, :] < counts[:, None]).astype(jnp.float32)
    masked = coupling * live_mask[:, :, None, None]
    cat_cols = jnp.transpose(masked, (0, 2, 1, 3)).reshape(SUBMAPS, NI, SLOTS * TILE)
    solved = jnp.einsum('bij,bjk->bik', interior_inverse, cat_cols, precision=TOP_ACCURACY)
    schur = jnp.einsum('bji,bjk->bik', cat_cols, solved, precision=TOP_ACCURACY)
    reduced = jnp.einsum('bij,bjk->bik', interior_inverse, interior_grad, precision=TOP_ACCURACY)
    pushed = jnp.einsum('bji,bjk->bik', cat_cols, reduced, precision=TOP_ACCURACY)
    positions = owner[lists].reshape(-1)
    schur_five = schur.reshape(SUBMAPS, SLOTS, TILE, SLOTS, TILE)
    diag_tiles = jnp.stack([schur_five[:, j, :, j, :] for j in range(SLOTS)], axis=1)
    diag_sum = jax.ops.segment_sum(diag_tiles.reshape(-1, TILE, TILE), positions, num_segments=NSEP)
    push_sum = jax.ops.segment_sum(pushed.reshape(-1, TILE, NRHS), positions, num_segments=NSEP)
    blockdiag = separator_hessian_blocks - diag_sum
    rhs_zero = sep_grad - push_sum
    factors = jnp.linalg.cholesky(blockdiag)

    def precond(resid):
        return jax.vmap(tile_solve)(factors, resid)

    def schur_operator_apply(input_vector):
        listed = input_vector[positions].reshape(SUBMAPS, SLOTS * TILE, NRHS)
        product = jnp.einsum('bij,bjk->bik', schur, listed, precision=TOP_ACCURACY)
        summed = jax.ops.segment_sum(product.reshape(-1, TILE, NRHS), positions, num_segments=NSEP)
        owned_portion = jnp.einsum('zvl,zlo->zvo', separator_hessian_blocks, input_vector, precision=TOP_ACCURACY)
        return owned_portion - summed
    z_zero = precond(rhs_zero)
    solution = z_zero
    direction = z_zero
    resid = rhs_zero - schur_operator_apply(z_zero)
    z_resid = precond(resid)
    quotient = jnp.sum(resid * z_resid) / jnp.sum(rhs_zero * z_zero)
    gamma_prev = 1.0
    for sweep in range(CHEB):
        gamma = 1.0 / (2.0 - quotient * gamma_prev)
        direction = quotient * gamma * gamma_prev * direction + 2.0 * gamma * z_resid
        solution = solution + direction
        resid = resid - schur_operator_apply(direction)
        if sweep + 1 < CHEB:
            z_resid = precond(resid)
        gamma_prev = gamma
    listed = solution[positions].reshape(SUBMAPS, SLOTS * TILE, NRHS)
    interior = reduced - jnp.einsum('bij,bjk->bik', solved, listed, precision=TOP_ACCURACY)
    return (interior, solution, resid)
```

```python
import jax
import jax.numpy as jnp
from jax import lax
from jax.experimental import pallas as pl
from jax.experimental.pallas import tpu as pltpu
from jax.sharding import PartitionSpec as P

F32 = jnp.float32
BF16 = jnp.bfloat16
SUB_DEV = 4
SLOTS = 4
TILE = 128
NI = 512
NRHS = 128
SEP_DEV = 4
PER_DEV = SUB_DEV * SLOTS
BLOCK = 32
VMEM_BYTES = 56 * 1024 * 1024

ROUTES = [(0, 0), (0, 1), (0, 2), (0, 3), (1, 0), (1, 1), (1, 2), (1, 3)]


def halves(x):
    high = x.astype(BF16)
    low = (x - high.astype(F32)).astype(BF16)
    return high, low


def dot3(a, b, dims=((1,), (0,))):
    (ah, al), (bh, bl) = a, b

    def one(x, y):
        return lax.dot_general(x, y, (dims, ((), ())), preferred_element_type=F32)

    return one(ah, bl) + one(al, bh) + one(ah, bh)


def params(**kw):
    return pltpu.CompilerParams(vmem_limit_bytes=VMEM_BYTES, **kw)


SMEM = pl.BlockSpec(memory_space=pltpu.SMEM)
VMEM = pl.BlockSpec(memory_space=pltpu.VMEM)


def walk_listings(place_ref, list_ref, owner_ref, count_ref, n_region, n_sub, first, last, visit):
    region = place_ref[0]

    def clear(i, carry):
        count_ref[i] = 0
        return carry

    lax.fori_loop(0, count_ref.shape[0], clear, 0)

    def step(n, carry):
        source = n // PER_DEV
        behind = 1 - source // n_sub
        pos = owner_ref[list_ref[n]]
        owner_dev = pos // SEP_DEV
        ahead = lax.rem(owner_dev // n_sub - (region - behind) + 2 * n_region, n_region)
        owner_sub = lax.rem(owner_dev, n_sub)
        key = (source * 2 + ahead) * n_sub + owner_sub
        rank = count_ref[key]
        count_ref[key] = rank + 1
        turn = lax.rem(owner_sub - lax.rem(source, n_sub) + n_sub, n_sub)
        slot = (ahead * n_sub + turn) * 2 + rank
        visit(n, source, behind, pos, ahead, owner_sub, slot)
        return carry

    lax.fori_loop(first, last, step, 0)


def plan_kernel(n_region, n_sub, place_ref, list_ref, owner_ref, target_ref, seen_ref, own_ref, count_ref):
    region, sub = place_ref[0], place_ref[1]

    def tile_at(pos):
        dev = pos // SEP_DEV
        side = lax.rem(dev // n_sub - region + 2 * n_region, n_region)
        side = jnp.where(side == 0, 0, jnp.where(side == 1, 2, 1))
        turn = lax.rem(sub - lax.rem(dev, n_sub) + n_sub, n_sub)
        return (side * n_sub + turn) * SEP_DEV + lax.rem(pos, SEP_DEV)

    def visit(n, source, behind, pos, ahead, owner_sub, slot):
        mine = (ahead == behind) & (owner_sub == sub)
        where = jnp.where(mine, slot, PER_DEV)
        target_ref[where] = lax.rem(pos, SEP_DEV)
        base = n - lax.rem(n, SLOTS)
        for k in range(1, SLOTS):
            other = owner_ref[list_ref[base + lax.rem(lax.rem(n, SLOTS) + k, SLOTS)]]
            seen_ref[where * (SLOTS - 1) + k - 1] = jnp.where(mine, tile_at(other), 0)

    walk_listings(place_ref, list_ref, owner_ref, count_ref, n_region, n_sub, 0, 2 * n_sub * PER_DEV, visit)
    begin = (n_sub + sub) * PER_DEV

    def mine(i, carry):
        own_ref[i] = tile_at(owner_ref[list_ref[begin + i]])
        return carry

    lax.fori_loop(0, PER_DEV, mine, 0)


def plan(place, near, owner, n_region, n_sub):
    shapes = (PER_DEV + 1, (PER_DEV + 1) * (SLOTS - 1), PER_DEV)
    return pl.pallas_call(
        lambda *refs: plan_kernel(n_region, n_sub, *refs),
        out_shape=tuple(jax.ShapeDtypeStruct((n,), jnp.int32) for n in shapes),
        in_specs=[SMEM] * 3,
        out_specs=(SMEM,) * 3,
        scratch_shapes=[pltpu.SMEM((4 * n_sub * n_sub,), jnp.int32)],
        compiler_params=params(),
        name="plan",
    )(place, near, owner)


def masked_cat(coupling_ref, live):
    parts = []
    for j in range(SLOTS):
        keep = (j < live).astype(F32)
        parts.append(halves(coupling_ref[0, j] * keep))
    return parts


def eliminate_kernel(
    n_region, n_sub, place_ref, list_ref, owner_ref, live_ref, inverse_ref, coupling_ref, grad_ref,
    solved_h_ref, solved_l_ref, reduced_ref, *rest
):
    chunks, (pay_ref, right_h, right_l, slot_ref, count_ref) = rest[:8], rest[8:]
    i = pl.program_id(0)
    begin = (n_sub + place_ref[1]) * PER_DEV

    @pl.when(i == 0)
    def _():
        def visit(n, source, behind, pos, ahead, owner_sub, slot):
            slot_ref[n - begin] = slot

        walk_listings(
            place_ref, list_ref, owner_ref, count_ref, n_region, n_sub, begin, begin + PER_DEV, visit
        )

    columns = masked_cat(coupling_ref, live_ref[i])
    for j in range(SLOTS):
        right_h[:, j * TILE : (j + 1) * TILE] = columns[j][0]
        right_l[:, j * TILE : (j + 1) * TILE] = columns[j][1]
    gh, gl = halves(grad_ref[0])
    right_h[:, SLOTS * TILE :] = gh
    right_l[:, SLOTS * TILE :] = gl
    left = halves(inverse_ref[0])
    both = dot3(left, (right_h[...], right_l[...]))
    reduced = both[:, SLOTS * TILE :]
    reduced_ref[0] = reduced
    rh, rl = halves(reduced)
    for j in range(SLOTS):
        sh, sl = halves(both[:, j * TILE : (j + 1) * TILE])
        solved_h_ref[0, :, j * TILE : (j + 1) * TILE] = sh
        solved_l_ref[0, :, j * TILE : (j + 1) * TILE] = sl
        pair = (jnp.concatenate([sh, rh], axis=1), jnp.concatenate([sl, rl], axis=1))
        pay_ref[slot_ref[i * SLOTS + j]] = dot3(columns[j], pair, ((0,), (0,)))

    @pl.when(i == SUB_DEV - 1)
    def _():
        for c in range(8):
            chunks[c][...] = pay_ref[2 * c : 2 * c + 2]


def eliminate(place, near, owner, live, interior_inverse, coupling, interior_grad, n_region, n_sub):
    span = SLOTS * TILE
    wide = TILE + NRHS
    step = lambda i: (i, 0, 0)
    whole = pl.BlockSpec((2, TILE, wide), lambda i: (0, 0, 0))
    return pl.pallas_call(
        lambda *refs: eliminate_kernel(n_region, n_sub, *refs),
        grid=(SUB_DEV,),
        out_shape=(
            jax.ShapeDtypeStruct((SUB_DEV, NI, span), BF16),
            jax.ShapeDtypeStruct((SUB_DEV, NI, span), BF16),
            jax.ShapeDtypeStruct((SUB_DEV, NI, NRHS), F32),
        )
        + (jax.ShapeDtypeStruct((2, TILE, wide), F32),) * 8,
        in_specs=[SMEM] * 4
        + [
            pl.BlockSpec((1, NI, NI), step),
            pl.BlockSpec((1, SLOTS, NI, TILE), lambda i: (i, 0, 0, 0)),
            pl.BlockSpec((1, NI, NRHS), step),
        ],
        out_specs=(
            pl.BlockSpec((1, NI, span), step),
            pl.BlockSpec((1, NI, span), step),
            pl.BlockSpec((1, NI, NRHS), step),
        )
        + (whole,) * 8,
        scratch_shapes=[
            pltpu.VMEM((PER_DEV, TILE, wide), F32),
            pltpu.VMEM((NI, span + NRHS), BF16),
            pltpu.VMEM((NI, span + NRHS), BF16),
            pltpu.SMEM((PER_DEV,), jnp.int32),
            pltpu.SMEM((4 * n_sub * n_sub,), jnp.int32),
        ],
        compiler_params=params(),
        name="eliminate",
    )(place, near, owner, live, interior_inverse, coupling, interior_grad)


def couple_kernel(
    n_region, n_sub, place_ref, list_ref, owner_ref, live_ref, coupling_ref, solved_h_ref, solved_l_ref, *rest
):
    chunks, (pay_ref, cat_h, cat_l, slot_ref, count_ref) = rest[:8], rest[8:]
    i = pl.program_id(0)
    begin = (n_sub + place_ref[1]) * PER_DEV

    @pl.when(i == 0)
    def _():
        def visit(n, source, behind, pos, ahead, owner_sub, slot):
            slot_ref[n - begin] = slot

        walk_listings(
            place_ref, list_ref, owner_ref, count_ref, n_region, n_sub, begin, begin + PER_DEV, visit
        )

    columns = masked_cat(coupling_ref, live_ref[i])
    for j in range(SLOTS):
        cat_h[:, j * TILE : (j + 1) * TILE] = columns[j][0]
        cat_l[:, j * TILE : (j + 1) * TILE] = columns[j][1]
    schur = dot3((cat_h[...], cat_l[...]), (solved_h_ref[0], solved_l_ref[0]), ((0,), (0,)))
    for j in range(SLOTS):
        slot = slot_ref[i * SLOTS + j]
        for k in range(1, SLOTS):
            other = (j + k) % SLOTS
            pay_ref[slot, :, (k - 1) * TILE : k * TILE] = schur[
                j * TILE : (j + 1) * TILE, other * TILE : (other + 1) * TILE
            ]

    @pl.when(i == SUB_DEV - 1)
    def _():
        for c in range(8):
            chunks[c][...] = pay_ref[2 * c : 2 * c + 2]


def couple(place, near, owner, live, coupling, solved_h, solved_l, n_region, n_sub):
    span = SLOTS * TILE
    wide = (SLOTS - 1) * TILE
    step = lambda i: (i, 0, 0)
    return pl.pallas_call(
        lambda *refs: couple_kernel(n_region, n_sub, *refs),
        grid=(SUB_DEV,),
        out_shape=(jax.ShapeDtypeStruct((2, TILE, wide), F32),) * 8,
        in_specs=[SMEM] * 4
        + [
            pl.BlockSpec((1, SLOTS, NI, TILE), lambda i: (i, 0, 0, 0)),
            pl.BlockSpec((1, NI, span), step),
            pl.BlockSpec((1, NI, span), step),
        ],
        out_specs=(pl.BlockSpec((2, TILE, wide), lambda i: (0, 0, 0)),) * 8,
        scratch_shapes=[
            pltpu.VMEM((PER_DEV, TILE, wide), F32),
            pltpu.VMEM((NI, span), BF16),
            pltpu.VMEM((NI, span), BF16),
            pltpu.SMEM((PER_DEV,), jnp.int32),
            pltpu.SMEM((4 * n_sub * n_sub,), jnp.int32),
        ],
        compiler_params=params(),
        cost_estimate=pl.CostEstimate(flops=3 * 2 * 4 * NI**3, bytes_accessed=12 << 20, transcendentals=0),
        name="couple",
    )(place, near, owner, live, coupling, solved_h, solved_l)


def lane_group(shape, axis):
    return lax.broadcasted_iota(jnp.int32, shape, axis) // BLOCK


def block_diagonal(w, kb):
    groups = TILE // BLOCK
    parts = []
    for m in range(groups):
        rows = w[m * BLOCK : (m + 1) * BLOCK]
        shift = ((m - kb) % groups) * BLOCK
        if shift:
            rows = pltpu.roll(rows, shift, 1)
        parts.append(jnp.where(lane_group(rows.shape, 1) == m, rows, 0.0))
    return parts


def packed_inverse(p):
    lane = lax.broadcasted_iota(jnp.int32, p.shape, 1)
    row_id = lax.broadcasted_iota(jnp.int32, p.shape, 0)
    group_base = lane // BLOCK * BLOCK
    for k in range(BLOCK):
        column = jnp.take_along_axis(p, group_base + k, axis=1)
        row = p[k : k + 1]
        recip = 1.0 / column[k : k + 1]
        at_k = lane == group_base + k
        new_row = jnp.where(at_k[:1], recip, row * recip)
        p = jnp.where(at_k, 0.0, p) - column * new_row
        p = jnp.where(row_id == k, new_row, p)
    return p


def batch_inverse(tiles):
    groups = TILE // BLOCK
    w = [
        jnp.concatenate([t[kb * BLOCK : (kb + 1) * BLOCK] for t in tiles], axis=0) for kb in range(groups)
    ]
    lane = lax.broadcasted_iota(jnp.int32, (TILE, TILE), 1)
    row_in = lax.broadcasted_iota(jnp.int32, (TILE, TILE), 0) % BLOCK
    for kb in range(groups):
        parts = block_diagonal(w[kb], kb)
        packed = packed_inverse(parts[0] + parts[1] + parts[2] + parts[3])
        inner = jnp.concatenate(
            [jnp.where(lane_group(packed.shape, 1) == m, packed, 0.0) for m in range(groups)], axis=0
        )
        in_block = lane // BLOCK == kb
        unit = (lane == kb * BLOCK + row_in).astype(F32)
        pivot = dot3(halves(inner), halves(jnp.where(in_block, unit, w[kb])))
        pivot_parts = halves(pivot)
        for other in range(groups):
            if other == kb:
                continue
            left = jnp.concatenate(block_diagonal(w[other], kb), axis=0)
            w[other] = jnp.where(in_block, 0.0, w[other]) - dot3(halves(left), pivot_parts)
        w[kb] = pivot
    return [
        jnp.concatenate([w[kb][m * BLOCK : (m + 1) * BLOCK] for kb in range(groups)], axis=0)
        for m in range(SEP_DEV)
    ]


def folded(x):
    return jnp.sum(x.reshape(-1, 8, x.shape[-1]), axis=0)


def start_kernel(target_ref, hess_ref, grad_ref, *rest):
    chunks, (inv_h_ref, inv_l_ref, u_ref, w_ref, norm_ref, sum_ref) = rest[:8], rest[8:]
    sum_ref[:, :, :TILE] = hess_ref[...]
    sum_ref[:, :, TILE:] = grad_ref[...]
    for a in range(PER_DEV):
        t = target_ref[a]
        sum_ref[t] = sum_ref[t] - chunks[a // 2][a % 2]
    inverses = batch_inverse([sum_ref[t, :, :TILE] for t in range(SEP_DEV)])
    norm = jnp.zeros((8, NRHS), F32)
    for t in range(SEP_DEV):
        inv_h, inv_l = halves(inverses[t])
        inv_h_ref[t] = inv_h
        inv_l_ref[t] = inv_l
        u = sum_ref[t, :, TILE:]
        w = dot3((inv_h, inv_l), halves(u))
        u_ref[t] = u
        w_ref[t] = w
        norm = norm + folded(u * w)
    norm_ref[...] = norm


def start(target, hess, grad, chunks):
    tile = jax.ShapeDtypeStruct((SEP_DEV, TILE, NRHS), F32)
    half = jax.ShapeDtypeStruct((SEP_DEV, TILE, TILE), BF16)
    return pl.pallas_call(
        start_kernel,
        out_shape=(half, half, tile, tile, jax.ShapeDtypeStruct((8, NRHS), F32)),
        in_specs=[SMEM] + [VMEM] * 10,
        out_specs=(VMEM,) * 5,
        scratch_shapes=[pltpu.VMEM((SEP_DEV, TILE, TILE + NRHS), F32)],
        compiler_params=params(),
        cost_estimate=pl.CostEstimate(flops=10**10, bytes_accessed=4 << 20, transcendentals=0),
        name="start",
    )(target, hess, grad, *chunks)


def apply_kernel(with_w, target_ref, seen_ref, inv_h_ref, inv_l_ref, *rest):
    offs, vs, outs = rest[:8], rest[8:20], rest[20:]
    u_ref = outs[0]
    v_h, v_l = outs[-2:]
    for c in range(12):
        h, l = halves(vs[c][...])
        v_h[c * SEP_DEV : (c + 1) * SEP_DEV] = h
        v_l[c * SEP_DEV : (c + 1) * SEP_DEV] = l
    u_ref[...] = jnp.zeros(u_ref.shape, F32)
    for a in range(PER_DEV):
        t = target_ref[a]
        ids = [seen_ref[a * (SLOTS - 1) + k] for k in range(SLOTS - 1)]
        right = tuple(jnp.concatenate([ref[n] for n in ids], axis=0) for ref in (v_h, v_l))
        u_ref[t] = u_ref[t] + dot3(halves(offs[a // 2][a % 2]), right)
    if with_w:
        w_ref, norm_ref = outs[1:3]
        norm = jnp.zeros((8, NRHS), F32)
        for t in range(SEP_DEV):
            u = u_ref[t]
            w = dot3((inv_h_ref[t], inv_l_ref[t]), halves(u))
            w_ref[t] = w
            norm = norm + folded(u * w)
        norm_ref[...] = norm


def apply(target, seen, inv_h, inv_l, offs, vs, with_w):
    tile = jax.ShapeDtypeStruct((SEP_DEV, TILE, NRHS), F32)
    outs = (tile, tile, jax.ShapeDtypeStruct((8, NRHS), F32)) if with_w else (tile,)
    return pl.pallas_call(
        lambda *refs: apply_kernel(with_w, *refs),
        out_shape=outs,
        in_specs=[SMEM] * 2 + [VMEM] * 22,
        out_specs=(VMEM,) * len(outs),
        scratch_shapes=[pltpu.VMEM((12 * SEP_DEV, TILE, NRHS), BF16)] * 2,
        compiler_params=params(),
        cost_estimate=pl.CostEstimate(flops=2 * 10**9, bytes_accessed=7 << 20, transcendentals=0),
        name="apply",
    )(target, seen, inv_h, inv_l, *offs, *vs)


def finish_kernel(own_ref, coef_ref, reduced_ref, solved_h_ref, solved_l_ref, u1_ref, u3_ref, *rest):
    groups, (interior_ref, x_ref, resid_ref, x_h, x_l) = rest[:24], rest[24:]
    for c in range(8):
        x = (
            coef_ref[0] * groups[c][...]
            + coef_ref[1] * groups[8 + c][...]
            + coef_ref[2] * groups[16 + c][...]
        )
        if c == 0:
            x_ref[...] = x
        h, l = halves(x)
        x_h[c * SEP_DEV : (c + 1) * SEP_DEV] = h
        x_l[c * SEP_DEV : (c + 1) * SEP_DEV] = l
    resid_ref[...] = coef_ref[3] * u3_ref[...] + coef_ref[4] * u1_ref[...]
    for i in range(SUB_DEV):
        ids = []
        for j in range(SLOTS):
            n = own_ref[i * SLOTS + j]
            ids.append(jnp.where(n >= 4 * SEP_DEV, n - 4 * SEP_DEV, n))
        right = tuple(jnp.concatenate([ref[n] for n in ids], axis=0) for ref in (x_h, x_l))
        interior_ref[i] = reduced_ref[i] - dot3((solved_h_ref[i], solved_l_ref[i]), right)


def finish(own, coefs, reduced, solved_h, solved_l, u1, u3, w0s, w1s, w2s):
    tile = jax.ShapeDtypeStruct((SEP_DEV, TILE, NRHS), F32)
    return pl.pallas_call(
        finish_kernel,
        out_shape=(jax.ShapeDtypeStruct((SUB_DEV, NI, NRHS), F32), tile, tile),
        in_specs=[SMEM] * 2 + [VMEM] * 29,
        out_specs=(VMEM,) * 3,
        scratch_shapes=[pltpu.VMEM((8 * SEP_DEV, TILE, NRHS), BF16)] * 2,
        compiler_params=params(),
        name="finish",
    )(own, coefs, reduced, solved_h, solved_l, u1, u3, *w0s, *w1s, *w2s)


def per_device(
    interior_inverse, coupling, interior_grad, separator_hessian_blocks, sep_grad, lists, owner, counts
):
    n_region = lax.axis_size("region")
    n_sub = lax.axis_size("sub")
    region = lax.axis_index("region")
    sub = lax.axis_index("sub")

    def shift(x, ahead, turn):
        pairs = [
            (r * n_sub + s, (r + ahead) % n_region * n_sub + (s + turn) % n_sub)
            for r in range(n_region)
            for s in range(n_sub)
        ]
        return lax.ppermute(x, ("region", "sub"), pairs)

    def exchange(chunks):
        return [chunks[0]] + [shift(chunks[c], *ROUTES[c]) for c in range(1, 8)]

    def spread(v):
        around = [v] + [shift(v, 0, turn) for turn in (1, 2, 3)]
        before = [shift(x, 1, 0) for x in around]
        after = [shift(x, -1, 0) for x in around]
        return around + before + after

    per_region = n_sub * SUB_DEV
    here = lax.dynamic_slice_in_dim(lists, region * per_region, per_region, 0)
    behind = lax.dynamic_slice_in_dim(lists, (region - 1) % n_region * per_region, per_region, 0)
    near = jnp.concatenate([behind, here], axis=0).reshape(-1)
    live = lax.dynamic_slice_in_dim(counts, (region * n_sub + sub) * SUB_DEV, SUB_DEV, 0)
    place = jnp.stack([region, sub]).astype(jnp.int32)
    key = (place, near, owner)

    solved_h, solved_l, reduced, *pay = eliminate(
        *key, live, interior_inverse, coupling, interior_grad, n_region, n_sub
    )
    arrived = exchange(pay)
    target, seen, own = plan(*key, n_region, n_sub)
    offs = couple(*key, live, coupling, solved_h, solved_l, n_region, n_sub)
    arrived, offs = lax.optimization_barrier((arrived, offs))
    offs = exchange(offs)
    inv_h, inv_l, u0, w0, norm0 = start(target, separator_hessian_blocks, sep_grad, arrived)
    w0s = spread(w0)
    u1, w1, norm1 = apply(target, seen, inv_h, inv_l, offs, w0s, True)
    norms = lax.all_gather(jnp.stack([jnp.sum(norm0, 0), jnp.sum(norm1, 0)]), ("region", "sub"))
    totals = jnp.sum(norms, axis=(0, 2))
    w1s = spread(w1)
    u2, w2, _ = apply(target, seen, inv_h, inv_l, offs, w1s, True)
    w2s = spread(w2)
    (u3,) = apply(target, seen, inv_h, inv_l, offs, w2s, False)
    q = totals[1] / totals[0]
    g1 = 1.0 / (2.0 - q)
    g2 = 1.0 / (2.0 - q * g1)
    back = q * g2 * g1
    coefs = jnp.stack(
        [
            1.0 + (1.0 + back) * g1 * q - 2.0 * g2 * g1 * q,
            (1.0 + back) * g1 * 2.0,
            4.0 * g2 * g1,
            4.0 * g1 * g2,
            -3.0 * q * g1 * g2,
        ]
    )
    near_parts = lambda ws: ws[:4] + ws[8:]
    return finish(
        own, coefs, reduced, solved_h, solved_l, u1, u3, near_parts(w0s), near_parts(w1s), near_parts(w2s)
    )


def solution(mesh):
    split3 = P(("region", "sub"), None, None)
    placed = (split3, P(("region", "sub"), None, None, None), split3, split3, split3, P(), P(), P())
    return jax.shard_map(
        per_device, mesh=mesh, in_specs=placed, out_specs=(split3, split3, split3), check_vma=False
    )
```

```python
import jax
import jax.numpy as jnp
from jax import lax
from jax.experimental import pallas as pl
from jax.experimental.pallas import tpu as pltpu
from jax.sharding import PartitionSpec as P

F32 = jnp.float32
BF16 = jnp.bfloat16
SUB_DEV = 4
SLOTS = 4
TILE = 128
NI = 512
NRHS = 128
SEP_DEV = 4
PER_DEV = SUB_DEV * SLOTS
BLOCK = 32
MIB = 1024 * 1024

PIECES = [
    [(0, 0)], [(0, 1)], [(0, 3)], [(0, 2)],
    [(1, 0)], [(1, 1), (1, 3)], [(1, 2)],
    [(2, 0), (2, 1), (2, 3), (2, 2)],
]
HALF = TILE // 2
PACKED = HALF + 8
NORM_ROWS = 8
SPREAD = SEP_DEV * TILE + NORM_ROWS


def halves(x):
    high = x.astype(BF16)
    low = (x - high.astype(F32)).astype(BF16)
    return high, low


def product(a, b):
    return lax.dot_general(a, b, (((1,), (0,)), ((), ())), preferred_element_type=F32)


def dot3(a, b):
    (ah, al), (bh, bl) = a, b
    return product(jnp.concatenate([ah, al, ah], 1), jnp.concatenate([bl, bh, bh], 0))


def dot4(stacked, paired):
    m, n = stacked.shape[0] // 2, paired.shape[1] // 2
    r = product(stacked, paired)
    return (r[m:, n:] + (r[m:, :n] + r[:m, n:])) + r[:m, :n]


def stack_halves(x):
    return jnp.concatenate(halves(x), axis=0)


def pair_halves(x):
    return jnp.concatenate(halves(x), axis=1)


def params(mib):
    return pltpu.CompilerParams(vmem_limit_bytes=mib * MIB)


SMEM = pl.BlockSpec(memory_space=pltpu.SMEM)
VMEM = pl.BlockSpec(memory_space=pltpu.VMEM)


def log2(n):
    assert n & (n - 1) == 0
    return n.bit_length() - 1


def send_slots(place_ref, list_ref, owner_ref, slot_ref, count_ref, n_region, n_sub):
    region, sub = place_ref[0], place_ref[1]
    begin = (n_sub + sub) * PER_DEV
    for c in range(2 * n_sub):
        count_ref[c] = 0

    def step(n, carry):
        dev = owner_ref[list_ref[begin + n]] >> log2(SEP_DEV)
        ahead = ((dev >> log2(n_sub)) - region) & (n_region - 1)
        turn = (dev - sub) & (n_sub - 1)
        key = ((ahead & 1) << log2(n_sub)) + turn
        rank = count_ref[key]
        count_ref[key] = rank + 1
        slot_ref[n] = key * 2 + rank
        return carry

    lax.fori_loop(0, PER_DEV, step, 0)


def plan_kernel(n_region, n_sub, place_ref, list_ref, owner_ref, target_ref, seen_ref, own_ref, next_ref):
    region, sub = place_ref[0], place_ref[1]
    me = region * n_sub + sub
    after = ((region + 1) & (n_region - 1)) * n_sub + sub

    def tile_at(pos):
        dev = pos >> log2(SEP_DEV)
        there = dev >> log2(n_sub)
        side = jnp.where(there == region, 0, jnp.where(there == (region ^ 1), 2, 1))
        turn = (sub - dev) & (n_sub - 1)
        return (side * n_sub + turn) * SEP_DEV + (pos & (SEP_DEV - 1))

    def source_step(source, carry):
        behind = 1 - (source >> log2(n_sub))
        turn = (sub - source) & (n_sub - 1)
        first = (behind * n_sub + turn) * 2

        def step(n, carry):
            slot, later = carry
            at = source * PER_DEV + n
            pos = owner_ref[list_ref[at]]
            dev = pos >> log2(SEP_DEV)
            mine = dev == me
            ahead = (dev == after) & (behind == 0)

            @pl.when(mine)
            def _():
                target_ref[slot] = pos & (SEP_DEV - 1)
                base = at & ~(SLOTS - 1)
                for k in range(1, SLOTS):
                    other = owner_ref[list_ref[base + ((n + k) & (SLOTS - 1))]]
                    seen_ref[slot * (SLOTS - 1) + k - 1] = tile_at(other)

            @pl.when(ahead)
            def _():
                next_ref[later] = pos & (SEP_DEV - 1)

            return jnp.where(mine, slot + 1, slot), jnp.where(ahead, later + 1, later)

        lax.fori_loop(0, PER_DEV, step, (first, turn * 2), unroll=4)
        return carry

    lax.fori_loop(0, 2 * n_sub, source_step, 0)
    begin = (n_sub + sub) * PER_DEV

    def mine(i, carry):
        own_ref[i] = tile_at(owner_ref[list_ref[begin + i]])
        return carry

    lax.fori_loop(0, PER_DEV, mine, 0)


def plan(place, near, owner, n_region, n_sub):
    shapes = (PER_DEV, PER_DEV * (SLOTS - 1), PER_DEV, 2 * n_sub)
    return pl.pallas_call(
        lambda *refs: plan_kernel(n_region, n_sub, *refs),
        out_shape=tuple(jax.ShapeDtypeStruct((n,), jnp.int32) for n in shapes),
        in_specs=[SMEM] * 3,
        out_specs=(SMEM,) * 4,
        compiler_params=params(2),
        cost_estimate=pl.CostEstimate(flops=2 * 10**9, bytes_accessed=8192, transcendentals=0),
        name="plan",
    )(place, near, owner)


def pack_symmetric(t):
    row = lax.broadcasted_iota(jnp.int32, (HALF, TILE), 0)
    lane = lax.broadcasted_iota(jnp.int32, (HALF, TILE), 1)
    top, low = t[:HALF], t[HALF:]
    body = jnp.where(row <= lane, top, pltpu.roll(low, HALF, 1))
    ends = jnp.sum(jnp.where(row == lane - HALF, low, 0.0), axis=0, keepdims=True)
    return jnp.concatenate([body, jnp.broadcast_to(ends, (8, TILE))], axis=0)


def unpack_symmetric(f):
    row = lax.broadcasted_iota(jnp.int32, (HALF, TILE), 0)
    lane = lax.broadcasted_iota(jnp.int32, (HALF, TILE), 1)
    body, ends = f[:HALF], f[HALF : HALF + 1]
    top = jnp.where(row < lane, body, 0.0)
    low = jnp.where((row > lane - HALF) & (lane >= HALF), pltpu.roll(body, HALF, 1), 0.0)
    part = jnp.concatenate([top, low], axis=0)
    ends = jnp.where(row == lane - HALF, ends, 0.0)
    diagonal = jnp.concatenate([jnp.where(row == lane, body, 0.0), ends], axis=0)
    return part + part.T + diagonal


def eliminate_kernel(
    n_region, n_sub, place_ref, list_ref, owner_ref, live_ref, inverse_ref, coupling_ref, grad_ref,
    solved_ref, reduced_ref, *rest
):
    chunks, (pay_ref, left_ref, right_ref, turned_ref, pair_ref, slot_ref, count_ref) = rest[:4], rest[4:]
    i = pl.program_id(0)
    span = SLOTS * TILE

    @pl.when(i == 0)
    def _():
        send_slots(place_ref, list_ref, owner_ref, slot_ref, count_ref, n_region, n_sub)

    live = live_ref[i]
    ah, al = halves(inverse_ref[0])
    left_ref[:, :NI] = ah
    left_ref[:, NI : 2 * NI] = al
    left_ref[:, 2 * NI :] = ah
    for j in range(SLOTS + 1):
        x = grad_ref[0] if j == SLOTS else coupling_ref[0, j] * (j < live).astype(F32)
        cols = slice(j * TILE, (j + 1) * TILE)
        high, low = halves(x)
        right_ref[:NI, cols] = low
        right_ref[NI : 2 * NI, cols] = high
        right_ref[2 * NI :, cols] = high
        if j < SLOTS:
            th, tl = halves(x.T)
            turned_ref[2 * j * TILE : (2 * j + 1) * TILE] = th
            turned_ref[(2 * j + 1) * TILE : (2 * j + 2) * TILE] = tl
    both = product(left_ref[...], right_ref[...])
    reduced = both[:, span:]
    reduced_ref[0] = reduced
    rh, rl = halves(reduced)
    pair_ref[:, TILE : 2 * TILE] = rh
    pair_ref[:, 3 * TILE :] = rl
    for j in range(SLOTS):
        cols = slice(j * TILE, (j + 1) * TILE)
        sh, sl = halves(both[:, cols])
        solved_ref[0, :NI, cols] = sh
        solved_ref[0, NI:, cols] = sl
        pair_ref[:, :TILE] = sh
        pair_ref[:, 2 * TILE : 3 * TILE] = sl
        result = dot4(turned_ref[2 * j * TILE : (2 * j + 2) * TILE], pair_ref[...])
        slot = slot_ref[i * SLOTS + j]
        pay_ref[slot, :PACKED] = pack_symmetric(result[:, :TILE])
        pay_ref[slot, PACKED:] = result[:, TILE:]

    @pl.when(i == SUB_DEV - 1)
    def _():
        for c in range(4):
            chunks[c][:2] = pay_ref[2 * c : 2 * c + 2]
            chunks[c][2:] = pay_ref[8 + 2 * c : 10 + 2 * c]


def eliminate(place, near, owner, live, interior_inverse, coupling, interior_grad, n_region, n_sub):
    span = SLOTS * TILE
    tall = PACKED + TILE
    step = lambda i: (i, 0, 0)
    return pl.pallas_call(
        lambda *refs: eliminate_kernel(n_region, n_sub, *refs),
        grid=(SUB_DEV,),
        out_shape=(
            jax.ShapeDtypeStruct((SUB_DEV, 2 * NI, span), BF16),
            jax.ShapeDtypeStruct((SUB_DEV, NI, NRHS), F32),
        )
        + (jax.ShapeDtypeStruct((4, tall, TILE), F32),) * 4,
        in_specs=[SMEM] * 4
        + [
            pl.BlockSpec((1, NI, NI), step),
            pl.BlockSpec((1, SLOTS, NI, TILE), lambda i: (i, 0, 0, 0)),
            pl.BlockSpec((1, NI, NRHS), step),
        ],
        out_specs=(pl.BlockSpec((1, 2 * NI, span), step), pl.BlockSpec((1, NI, NRHS), step))
        + (pl.BlockSpec((4, tall, TILE), lambda i: (0, 0, 0)),) * 4,
        scratch_shapes=[
            pltpu.VMEM((PER_DEV, tall, TILE), F32),
            pltpu.VMEM((NI, 3 * NI), BF16),
            pltpu.VMEM((3 * NI, span + NRHS), BF16),
            pltpu.VMEM((2 * span, NI), BF16),
            pltpu.VMEM((NI, 2 * (TILE + NRHS)), BF16),
            pltpu.SMEM((PER_DEV,), jnp.int32),
            pltpu.SMEM((2 * n_sub,), jnp.int32),
        ],
        compiler_params=params(56),
        name="eliminate",
    )(place, near, owner, live, interior_inverse, coupling, interior_grad)


def couple_kernel(
    n_region, n_sub, place_ref, list_ref, owner_ref, live_ref, coupling_ref, solved_ref, *rest
):
    chunks, (pay_ref, turned_ref, right_ref, slot_ref, count_ref) = rest[:8], rest[8:]
    i = pl.program_id(0)

    @pl.when(i == 0)
    def _():
        send_slots(place_ref, list_ref, owner_ref, slot_ref, count_ref, n_region, n_sub)

    live = live_ref[i]
    for j in range(SLOTS):
        rows = slice(j * TILE, (j + 1) * TILE)
        th, tl = halves((coupling_ref[0, j] * (j < live).astype(F32)).T)
        turned_ref[rows, :NI] = th
        turned_ref[rows, NI : 2 * NI] = tl
        turned_ref[rows, 2 * NI :] = th
    right_ref[:NI] = solved_ref[0, NI:]
    right_ref[NI : 2 * NI] = solved_ref[0, :NI]
    right_ref[2 * NI :] = solved_ref[0, :NI]
    schur = product(turned_ref[...], right_ref[...])
    for j in range(SLOTS):
        slot = slot_ref[i * SLOTS + j]
        for k in range(1, SLOTS):
            other = (j + k) % SLOTS
            pay_ref[slot, :, (k - 1) * TILE : k * TILE] = schur[
                j * TILE : (j + 1) * TILE, other * TILE : (other + 1) * TILE
            ]

    @pl.when(i == SUB_DEV - 1)
    def _():
        for c in range(8):
            chunks[c][...] = pay_ref[2 * c : 2 * c + 2]


def couple(place, near, owner, live, coupling, solved, n_region, n_sub):
    span = SLOTS * TILE
    wide = (SLOTS - 1) * TILE
    return pl.pallas_call(
        lambda *refs: couple_kernel(n_region, n_sub, *refs),
        grid=(SUB_DEV,),
        out_shape=(jax.ShapeDtypeStruct((2, TILE, wide), F32),) * 8,
        in_specs=[SMEM] * 4
        + [
            pl.BlockSpec((1, SLOTS, NI, TILE), lambda i: (i, 0, 0, 0)),
            pl.BlockSpec((1, 2 * NI, span), lambda i: (i, 0, 0)),
        ],
        out_specs=(pl.BlockSpec((2, TILE, wide), lambda i: (0, 0, 0)),) * 8,
        scratch_shapes=[
            pltpu.VMEM((PER_DEV, TILE, wide), F32),
            pltpu.VMEM((span, 3 * NI), BF16),
            pltpu.VMEM((3 * NI, span), BF16),
            pltpu.SMEM((PER_DEV,), jnp.int32),
            pltpu.SMEM((2 * n_sub,), jnp.int32),
        ],
        compiler_params=params(32),
        cost_estimate=pl.CostEstimate(flops=8 * 10**9, bytes_accessed=12 * MIB, transcendentals=0),
        name="couple",
    )(place, near, owner, live, coupling, solved)


def lane_group(shape, axis):
    return lax.broadcasted_iota(jnp.int32, shape, axis) // BLOCK


def block_diagonal(w, kb):
    groups = TILE // BLOCK
    parts = []
    for m in range(groups):
        rows = w[m * BLOCK : (m + 1) * BLOCK]
        shift = ((m - kb) % groups) * BLOCK
        if shift:
            rows = pltpu.roll(rows, shift, 1)
        parts.append(jnp.where(lane_group(rows.shape, 1) == m, rows, 0.0))
    return parts


def packed_inverse(p):
    lane = lax.broadcasted_iota(jnp.int32, p.shape, 1)
    row_id = lax.broadcasted_iota(jnp.int32, p.shape, 0)
    group_base = lane // BLOCK * BLOCK
    for k in range(0, BLOCK, 2):
        first = jnp.take_along_axis(p, group_base + k, axis=1)
        second = jnp.take_along_axis(p, group_base + (k + 1), axis=1)
        a, c = first[k : k + 1], first[k + 1 : k + 2]
        b, d = second[k : k + 1], second[k + 1 : k + 2]
        recip = 1.0 / (a * d - b * c)
        at_first = lane == group_base + k
        at_second = lane == group_base + (k + 1)
        row0 = jnp.where(at_first[:1], 1.0, jnp.where(at_second[:1], 0.0, p[k : k + 1]))
        row1 = jnp.where(at_first[:1], 0.0, jnp.where(at_second[:1], 1.0, p[k + 1 : k + 2]))
        new0 = (d * row0 - b * row1) * recip
        new1 = (a * row1 - c * row0) * recip
        p = jnp.where(at_first | at_second, 0.0, p) - first * new0 - second * new1
        p = jnp.where(row_id == k, new0, jnp.where(row_id == k + 1, new1, p))
    return p


def batch_inverse(tiles):
    groups = TILE // BLOCK
    w = [
        jnp.concatenate([t[kb * BLOCK : (kb + 1) * BLOCK] for t in tiles], axis=0) for kb in range(groups)
    ]
    lane = lax.broadcasted_iota(jnp.int32, (TILE, TILE), 1)
    row_in = lax.broadcasted_iota(jnp.int32, (TILE, TILE), 0) % BLOCK
    for kb in range(groups):
        parts = block_diagonal(w[kb], kb)
        packed = packed_inverse(parts[0] + parts[1] + parts[2] + parts[3])
        inner = jnp.concatenate(
            [jnp.where(lane_group(packed.shape, 1) == m, packed, 0.0) for m in range(groups)], axis=0
        )
        in_block = lane // BLOCK == kb
        unit = (lane == kb * BLOCK + row_in).astype(F32)
        pivot = dot3(halves(inner), halves(jnp.where(in_block, unit, w[kb])))
        pivot_parts = halves(pivot)
        for other in range(groups):
            if other == kb:
                continue
            left = jnp.concatenate(block_diagonal(w[other], kb), axis=0)
            w[other] = jnp.where(in_block, 0.0, w[other]) - dot3(halves(left), pivot_parts)
        w[kb] = pivot
    return [
        jnp.concatenate([w[kb][m * BLOCK : (m + 1) * BLOCK] for kb in range(groups)], axis=0)
        for m in range(SEP_DEV)
    ]


def folded(x):
    return jnp.sum(x.reshape(-1, 8, x.shape[-1]), axis=0)


def gather_kernel(target_ref, next_ref, c0, c1, c2, c3, here_ref, next_sum_ref):
    here_ref[...] = jnp.zeros(here_ref.shape, F32)
    next_sum_ref[...] = jnp.zeros(here_ref.shape, F32)
    for turn, chunk in enumerate((c0, c1, c2, c3)):
        for rank in range(2):
            t = target_ref[2 * turn + rank]
            here_ref[t] = here_ref[t] + chunk[rank]
            t = next_ref[2 * turn + rank]
            next_sum_ref[t] = next_sum_ref[t] + chunk[2 + rank]


def gather(target, later, chunks):
    total = jax.ShapeDtypeStruct((SEP_DEV, PACKED + TILE, TILE), F32)
    return pl.pallas_call(
        gather_kernel,
        out_shape=(total, total),
        in_specs=[SMEM] * 2 + [VMEM] * 4,
        out_specs=(VMEM,) * 2,
        compiler_params=params(8),
        name="gather",
    )(target, later, *chunks)


def invert_kernel(hess_ref, grad_ref, here_ref, got_ref, inv_ref, u_ref):
    tiles = []
    for t in range(SEP_DEV):
        total = here_ref[t] + got_ref[t]
        tiles.append(hess_ref[t] - unpack_symmetric(total[:PACKED]))
        u_ref[t] = grad_ref[t] - total[PACKED:]
    inverses = batch_inverse(tiles)
    for t in range(SEP_DEV):
        inv_ref[t] = stack_halves(inverses[t])


def invert(hess, grad, here, got):
    return pl.pallas_call(
        invert_kernel,
        out_shape=(
            jax.ShapeDtypeStruct((SEP_DEV, 2 * TILE, TILE), BF16),
            jax.ShapeDtypeStruct((SEP_DEV, TILE, NRHS), F32),
        ),
        in_specs=[VMEM] * 4,
        out_specs=(VMEM,) * 2,
        compiler_params=params(14),
        cost_estimate=pl.CostEstimate(flops=10**10, bytes_accessed=4 * MIB, transcendentals=0),
        name="invert",
    )(hess, grad, here, got)


def precondition(inv_ref, u_ref, earlier, w_ref):
    norm = jnp.zeros((8, NRHS), F32)
    for t in range(SEP_DEV):
        u = u_ref[t]
        w = dot4(inv_ref[t], pair_halves(u))
        w_ref[t * TILE : (t + 1) * TILE] = w
        norm = norm + folded(u * w)
    norm = jnp.sum(norm, axis=0, keepdims=True)
    row = lax.broadcasted_iota(jnp.int32, (NORM_ROWS, NRHS), 0)
    w_ref[SEP_DEV * TILE :] = jnp.where(row == 0, norm if earlier is None else earlier, jnp.where(row == 1, norm, 0.0))


WIDE = jax.ShapeDtypeStruct((SPREAD, NRHS), F32)


def begin(inv, u):
    return pl.pallas_call(
        lambda inv_ref, u_ref, w_ref: precondition(inv_ref, u_ref, None, w_ref),
        out_shape=WIDE,
        in_specs=[VMEM] * 2,
        out_specs=VMEM,
        compiler_params=params(8),
        name="begin",
    )(inv, u)


def lay_out(pieces, v_ref, sides):
    for piece, spots in zip(pieces, PIECES):
        for n, (side, turn) in enumerate(spots):
            if side not in sides:
                continue
            for t in range(SEP_DEV):
                where = (sides.index(side) * 4 + turn) * SEP_DEV + t
                rows = n * SPREAD + t * TILE
                v_ref[where] = pair_halves(piece[rows : rows + TILE])


def scatter(target_ref, seen_ref, offs, v_ref, u_ref):
    u_ref[...] = jnp.zeros(u_ref.shape, F32)
    for a in range(PER_DEV):
        t = target_ref[a]
        right = [v_ref[seen_ref[a * (SLOTS - 1) + k]] for k in range(SLOTS - 1)]
        off = offs[a // 2][a % 2] if a < 8 else offs[4][a - 8]
        u_ref[t] = u_ref[t] + dot4(stack_halves(off), jnp.concatenate(right, axis=0))


def apply_kernel(target_ref, seen_ref, inv_ref, *rest):
    offs, pieces, (u_ref, w_ref, v_ref) = rest[:5], rest[5:13], rest[13:]
    lay_out(pieces, v_ref, (0, 1, 2))
    scatter(target_ref, seen_ref, offs, v_ref, u_ref)
    precondition(inv_ref, u_ref, pieces[0][SEP_DEV * TILE : SEP_DEV * TILE + 1], w_ref)


def apply(target, seen, inv, offs, pieces):
    tile = jax.ShapeDtypeStruct((SEP_DEV, TILE, NRHS), F32)
    return pl.pallas_call(
        apply_kernel,
        out_shape=(tile, WIDE),
        in_specs=[SMEM] * 2 + [VMEM] * 14,
        out_specs=(VMEM,) * 2,
        scratch_shapes=[pltpu.VMEM((12 * SEP_DEV, TILE, 2 * NRHS), BF16)],
        compiler_params=params(16),
        cost_estimate=pl.CostEstimate(flops=2 * 10**9, bytes_accessed=7 * MIB, transcendentals=0),
        name="apply",
    )(target, seen, inv, *offs, *pieces)


def listed(own_ref, v_ref, i):
    tiles = []
    for j in range(SLOTS):
        n = own_ref[i * SLOTS + j]
        tiles.append(v_ref[n])
    return jnp.concatenate(tiles, axis=0)


def ahead_kernel(own_ref, solved_ref, *rest):
    first, second, (ya_ref, yb_ref, v_ref) = rest[:8], rest[8:16], rest[16:]
    for pieces, y_ref in ((first, ya_ref), (second, yb_ref)):
        lay_out(pieces, v_ref, (0, 1, 2))
        for i in range(SUB_DEV):
            y_ref[i] = dot4(solved_ref[i], listed(own_ref, v_ref, i))


def ahead(own, solved, w0s, w1s):
    y = jax.ShapeDtypeStruct((SUB_DEV, NI, NRHS), F32)
    return pl.pallas_call(
        ahead_kernel,
        out_shape=(y, y),
        in_specs=[SMEM] + [VMEM] * 17,
        out_specs=(VMEM,) * 2,
        scratch_shapes=[pltpu.VMEM((12 * SEP_DEV, TILE, 2 * NRHS), BF16)],
        compiler_params=params(28),
        cost_estimate=pl.CostEstimate(flops=8 * 10**9, bytes_accessed=14 * MIB, transcendentals=0),
        name="ahead",
    )(own, solved, *w0s, *w1s)


def finish_kernel(
    target_ref, seen_ref, own_ref, norm_ref, solved_ref, reduced_ref, ya_ref, yb_ref, u1_ref, w0_ref, w1_ref, *rest
):
    offs, pieces, (interior_ref, x_ref, resid_ref, v_ref, u_ref) = rest[:5], rest[5:13], rest[13:]
    whole = lambda x: jnp.sum(jnp.sum(x, axis=0, keepdims=True), axis=1, keepdims=True)
    q = whole(norm_ref[1:2]) / whole(norm_ref[:1])
    g1 = 1.0 / (2.0 - q)
    g2 = 1.0 / (2.0 - q * g1)
    back = q * g2 * g1
    c0 = 1.0 + (1.0 + back) * g1 * q - 2.0 * g2 * g1 * q
    c1 = (1.0 + back) * g1 * 2.0
    c2 = 4.0 * g2 * g1
    lay_out(pieces, v_ref, (0, 1, 2))
    for i in range(SUB_DEV):
        y = dot4(solved_ref[i], listed(own_ref, v_ref, i))
        interior_ref[i] = reduced_ref[i] - (c0 * ya_ref[i] + c1 * yb_ref[i] + c2 * y)
    scatter(target_ref, seen_ref, offs, v_ref, u_ref)
    for t in range(SEP_DEV):
        rows = slice(t * TILE, (t + 1) * TILE)
        x_ref[t] = c0 * w0_ref[rows] + c1 * w1_ref[rows] + c2 * pieces[0][rows]
        resid_ref[t] = g1 * g2 * (4.0 * u_ref[t] - 3.0 * q * u1_ref[t])


def finish(target, seen, own, norms, solved, reduced, ya, yb, u1, w0, w1, offs, w2s):
    tile = jax.ShapeDtypeStruct((SEP_DEV, TILE, NRHS), F32)
    return pl.pallas_call(
        finish_kernel,
        out_shape=(jax.ShapeDtypeStruct((SUB_DEV, NI, NRHS), F32), tile, tile),
        in_specs=[SMEM] * 3 + [VMEM] * 21,
        out_specs=(VMEM,) * 3,
        scratch_shapes=[
            pltpu.VMEM((12 * SEP_DEV, TILE, 2 * NRHS), BF16),
            pltpu.VMEM((SEP_DEV, TILE, NRHS), F32),
        ],
        compiler_params=params(30),
        name="finish",
    )(target, seen, own, norms, solved, reduced, ya, yb, u1, w0, w1, *offs, *w2s)


def per_device(
    interior_inverse, coupling, interior_grad, separator_hessian_blocks, sep_grad, lists, owner, counts
):
    n_region = lax.axis_size("region")
    n_sub = lax.axis_size("sub")
    region = lax.axis_index("region")
    sub = lax.axis_index("sub")
    both = ("region", "sub")

    def shift(x, ahead, turn):
        pairs = [
            (r * n_sub + s, (r + ahead) % n_region * n_sub + (s + turn) % n_sub)
            for r in range(n_region)
            for s in range(n_sub)
        ]
        return lax.ppermute(x, both, pairs)

    def swap(x, partner):
        pairs = [(r * n_sub + s, partner(r) * n_sub + s) for r in range(n_region) for s in range(n_sub)]
        return lax.ppermute(x, both, pairs)

    def across(x):
        return swap(x, lambda r: (r + 1 if r % 2 else r - 1) % n_region)

    def mate(x):
        return swap(x, lambda r: r ^ 1)

    def add_over(x, steps):
        for step in steps:
            x = x + swap(x, lambda r: r ^ step)
        return x

    def around(chunks):
        return [chunks[0]] + [shift(chunks[turn], 0, turn) for turn in range(1, n_sub)]

    def spread(v, small=None, steps=((), ())):
        z1, z3, z2 = (shift(v, 0, turn) for turn in (1, 3, 2))
        if small is None:
            small = sum(x[SEP_DEV * TILE :] for x in (v, z1, z3, z2))
        pair = jnp.concatenate([z1, z3], axis=0)
        pair_across = across(pair)
        if steps[0]:
            small, z2 = lax.optimization_barrier((small, z2))
            small = add_over(small, steps[0])
        z2_across = across(z2)
        all_mate = mate(jnp.concatenate([v, z1, z3, z2], axis=0))
        if steps[1]:
            small, all_mate = lax.optimization_barrier((small, all_mate))
            small = add_over(small, steps[1])
        return [v, z1, z3, z2, across(v), pair_across, z2_across, all_mate], small

    per_region = n_sub * SUB_DEV
    here = lax.dynamic_slice_in_dim(lists, region * per_region, per_region, 0)
    behind = lax.dynamic_slice_in_dim(lists, (region - 1) % n_region * per_region, per_region, 0)
    near = jnp.concatenate([behind, here], axis=0).reshape(-1)
    live = lax.dynamic_slice_in_dim(counts, (region * n_sub + sub) * SUB_DEV, SUB_DEV, 0)
    place = jnp.stack([region, sub]).astype(jnp.int32)
    key = (place, near, owner)

    solved, reduced, *pay = eliminate(*key, live, interior_inverse, coupling, interior_grad, n_region, n_sub)
    arrived = around(pay)
    target, seen, own, later = plan(*key, n_region, n_sub)
    offs = couple(*key, live, coupling, solved, n_region, n_sub)
    arrived, offs = lax.optimization_barrier((arrived, offs))
    far = around(offs[4:])
    here, following = gather(target, later, arrived)
    got = shift(following, 1, 0)
    inv, u0 = invert(separator_hessian_blocks, sep_grad, here, got)
    u0, far = lax.optimization_barrier((u0, far))
    forwarded = shift(jnp.concatenate(far, axis=0), 1, 0)
    w0 = begin(inv, u0)
    w0s, _ = spread(w0, u0[0, :NORM_ROWS])
    offs = around(offs[:4]) + [forwarded]
    u1, w1 = apply(target, seen, inv, offs, w0s)
    w1s, norms = spread(w1, None, ((), (1, 2)))
    u2, w2 = apply(target, seen, inv, offs, w1s)
    w2s, norms = spread(w2, norms, ((4,), (8, 16)))
    ya, yb = ahead(own, solved, w0s, w1s)
    return finish(target, seen, own, norms, solved, reduced, ya, yb, u1, w0, w1, offs, w2s)


def solution(mesh):
    split3 = P(("region", "sub"), None, None)
    placed = (split3, P(("region", "sub"), None, None, None), split3, split3, split3, P(), P(), P())
    return jax.shard_map(
        per_device, mesh=mesh, in_specs=placed, out_specs=(split3, split3, split3), check_vma=False
    )
```

```python
import jax
import jax.numpy as jnp
from jax import lax
from jax.experimental import pallas as pl
from jax.experimental.pallas import tpu as pltpu
from jax.sharding import PartitionSpec as P

F32 = jnp.float32
BF16 = jnp.bfloat16
SUB_DEV = 4
SLOTS = 4
TILE = 128
NI = 512
NRHS = 128
SEP_DEV = 4
PER_DEV = SUB_DEV * SLOTS
BLOCK = 32
MIB = 1024 * 1024

PIECES = [
    [(0, 0)], [(0, 1)], [(0, 3)], [(0, 2)],
    [(1, 0)], [(1, 1), (1, 3)], [(1, 2)],
    [(2, 0), (2, 1), (2, 3), (2, 2)],
]
HALF = TILE // 2
PACKED = HALF + 8
NORM_ROWS = 8
SPREAD = SEP_DEV * TILE + NORM_ROWS


def halves(x):
    high = x.astype(BF16)
    low = (x - high.astype(F32)).astype(BF16)
    return high, low


def product(a, b):
    return lax.dot_general(a, b, (((1,), (0,)), ((), ())), preferred_element_type=F32)


def dot3(a, b):
    (ah, al), (bh, bl) = a, b
    return product(jnp.concatenate([ah, al, ah], 1), jnp.concatenate([bl, bh, bh], 0))


def dot4(stacked, paired):
    m, n = stacked.shape[0] // 2, paired.shape[1] // 2
    r = product(stacked, paired)
    return (r[m:, n:] + (r[m:, :n] + r[:m, n:])) + r[:m, :n]


def stack_halves(x):
    return jnp.concatenate(halves(x), axis=0)


def pair_halves(x):
    return jnp.concatenate(halves(x), axis=1)


def params(mib):
    return pltpu.CompilerParams(vmem_limit_bytes=mib * MIB)


SMEM = pl.BlockSpec(memory_space=pltpu.SMEM)
VMEM = pl.BlockSpec(memory_space=pltpu.VMEM)


def log2(n):
    assert n & (n - 1) == 0
    return n.bit_length() - 1


def send_slots(list_ref, owner_ref, slot_ref, count_ref, n_region, n_sub):
    region, sub = lax.axis_index("region"), lax.axis_index("sub")
    begin = (n_sub + sub) * PER_DEV
    for c in range(2 * n_sub):
        count_ref[c] = 0

    def step(n, carry):
        dev = owner_ref[list_ref[begin + n]] >> log2(SEP_DEV)
        ahead = ((dev >> log2(n_sub)) - region) & (n_region - 1)
        turn = (dev - sub) & (n_sub - 1)
        key = ((ahead & 1) << log2(n_sub)) + turn
        rank = count_ref[key]
        count_ref[key] = rank + 1
        slot_ref[n] = key * 2 + rank
        return carry

    lax.fori_loop(0, PER_DEV, step, 0)


def plan_kernel(n_region, n_sub, list_ref, owner_ref, target_ref, seen_ref, own_ref, next_ref):
    region, sub = lax.axis_index("region"), lax.axis_index("sub")
    me = region * n_sub + sub
    after = ((region + 1) & (n_region - 1)) * n_sub + sub

    def tile_at(pos):
        dev = pos >> log2(SEP_DEV)
        there = dev >> log2(n_sub)
        side = jnp.where(there == region, 0, jnp.where(there == (region ^ 1), 2, 1))
        turn = (sub - dev) & (n_sub - 1)
        return (side * n_sub + turn) * SEP_DEV + (pos & (SEP_DEV - 1))

    def source_step(source, carry):
        behind = 1 - (source >> log2(n_sub))
        turn = (sub - source) & (n_sub - 1)
        first = (behind * n_sub + turn) * 2

        def step(n, carry):
            slot, later = carry
            at = source * PER_DEV + n
            pos = owner_ref[list_ref[at]]
            dev = pos >> log2(SEP_DEV)
            mine = dev == me
            ahead = (dev == after) & (behind == 0)

            @pl.when(mine)
            def _():
                target_ref[slot] = pos & (SEP_DEV - 1)
                base = at & ~(SLOTS - 1)
                for k in range(1, SLOTS):
                    other = owner_ref[list_ref[base + ((n + k) & (SLOTS - 1))]]
                    seen_ref[slot * (SLOTS - 1) + k - 1] = tile_at(other)

            @pl.when(ahead)
            def _():
                next_ref[later] = pos & (SEP_DEV - 1)

            return jnp.where(mine, slot + 1, slot), jnp.where(ahead, later + 1, later)

        lax.fori_loop(0, PER_DEV, step, (first, turn * 2), unroll=4)
        return carry

    lax.fori_loop(0, 2 * n_sub, source_step, 0)
    begin = (n_sub + sub) * PER_DEV

    def mine(i, carry):
        own_ref[i] = tile_at(owner_ref[list_ref[begin + i]])
        return carry

    lax.fori_loop(0, PER_DEV, mine, 0)


def plan(near, owner, n_region, n_sub):
    shapes = (PER_DEV, PER_DEV * (SLOTS - 1), PER_DEV, 2 * n_sub)
    return pl.pallas_call(
        lambda *refs: plan_kernel(n_region, n_sub, *refs),
        out_shape=tuple(jax.ShapeDtypeStruct((n,), jnp.int32) for n in shapes),
        in_specs=[SMEM] * 2,
        out_specs=(SMEM,) * 4,
        compiler_params=params(2),
        cost_estimate=pl.CostEstimate(flops=2 * 10**9, bytes_accessed=8192, transcendentals=0),
        name="plan",
    )(near, owner)


def pack_symmetric(t):
    row = lax.broadcasted_iota(jnp.int32, (HALF, TILE), 0)
    lane = lax.broadcasted_iota(jnp.int32, (HALF, TILE), 1)
    top, low = t[:HALF], t[HALF:]
    body = jnp.where(row <= lane, top, pltpu.roll(low, HALF, 1))
    ends = jnp.sum(jnp.where(row == lane - HALF, low, 0.0), axis=0, keepdims=True)
    return jnp.concatenate([body, jnp.broadcast_to(ends, (8, TILE))], axis=0)


def unpack_symmetric(f):
    row = lax.broadcasted_iota(jnp.int32, (HALF, TILE), 0)
    lane = lax.broadcasted_iota(jnp.int32, (HALF, TILE), 1)
    body, ends = f[:HALF], f[HALF : HALF + 1]
    top = jnp.where(row < lane, body, 0.0)
    low = jnp.where((row > lane - HALF) & (lane >= HALF), pltpu.roll(body, HALF, 1), 0.0)
    part = jnp.concatenate([top, low], axis=0)
    ends = jnp.where(row == lane - HALF, ends, 0.0)
    diagonal = jnp.concatenate([jnp.where(row == lane, body, 0.0), ends], axis=0)
    return part + part.T + diagonal


def eliminate_kernel(
    n_region, n_sub, list_ref, owner_ref, live_ref, inverse_ref, coupling_ref, grad_ref,
    solved_ref, reduced_ref, *rest
):
    chunks, (pay_ref, left_ref, right_ref, turned_ref, slot_ref, count_ref) = rest[:4], rest[4:]
    i = pl.program_id(0)
    span = SLOTS * TILE

    @pl.when(i == 0)
    def _():
        send_slots(list_ref, owner_ref, slot_ref, count_ref, n_region, n_sub)

    live = live_ref[(lax.axis_index("region") * n_sub + lax.axis_index("sub")) * SUB_DEV + i]
    ah, al = halves(inverse_ref[0])
    left_ref[:, :NI] = ah
    left_ref[:, NI : 2 * NI] = al
    left_ref[:, 2 * NI :] = ah
    for j in range(SLOTS + 1):
        x = grad_ref[0] if j == SLOTS else coupling_ref[0, j] * (j < live).astype(F32)
        cols = slice(j * TILE, (j + 1) * TILE)
        high, low = halves(x)
        right_ref[:NI, cols] = low
        right_ref[NI : 2 * NI, cols] = high
        right_ref[2 * NI :, cols] = high
        if j < SLOTS:
            th, tl = halves(x.T)
            turned_ref[2 * j * TILE : (2 * j + 1) * TILE] = th
            turned_ref[(2 * j + 1) * TILE : (2 * j + 2) * TILE] = tl
    both = product(left_ref[...], right_ref[...])
    reduced = both[:, span:]
    reduced_ref[0] = reduced
    pushed = product(turned_ref[...], pair_halves(reduced))
    for j in range(SLOTS):
        cols = slice(j * TILE, (j + 1) * TILE)
        sh, sl = halves(both[:, cols])
        solved_ref[0, :NI, cols] = sh
        solved_ref[0, NI:, cols] = sl
        slot = slot_ref[i * SLOTS + j]
        diagonal = dot4(turned_ref[2 * j * TILE : (2 * j + 2) * TILE], jnp.concatenate([sh, sl], axis=1))
        pay_ref[slot, :PACKED] = pack_symmetric(diagonal)
        part = pushed[2 * j * TILE : (2 * j + 2) * TILE]
        pay_ref[slot, PACKED:] = (part[TILE:, NRHS:] + (part[TILE:, :NRHS] + part[:TILE, NRHS:])) + part[:TILE, :NRHS]

    @pl.when(i == SUB_DEV - 1)
    def _():
        for c in range(4):
            chunks[c][:2] = pay_ref[2 * c : 2 * c + 2]
            chunks[c][2:] = pay_ref[8 + 2 * c : 10 + 2 * c]


def eliminate(near, owner, live, interior_inverse, coupling, interior_grad, n_region, n_sub):
    span = SLOTS * TILE
    tall = PACKED + TILE
    step = lambda i: (i, 0, 0)
    return pl.pallas_call(
        lambda *refs: eliminate_kernel(n_region, n_sub, *refs),
        grid=(SUB_DEV,),
        out_shape=(
            jax.ShapeDtypeStruct((SUB_DEV, 2 * NI, span), BF16),
            jax.ShapeDtypeStruct((SUB_DEV, NI, NRHS), F32),
        )
        + (jax.ShapeDtypeStruct((4, tall, TILE), F32),) * 4,
        in_specs=[SMEM] * 3
        + [
            pl.BlockSpec((1, NI, NI), step),
            pl.BlockSpec((1, SLOTS, NI, TILE), lambda i: (i, 0, 0, 0)),
            pl.BlockSpec((1, NI, NRHS), step),
        ],
        out_specs=(pl.BlockSpec((1, 2 * NI, span), step), pl.BlockSpec((1, NI, NRHS), step))
        + (pl.BlockSpec((4, tall, TILE), lambda i: (0, 0, 0)),) * 4,
        scratch_shapes=[
            pltpu.VMEM((PER_DEV, tall, TILE), F32),
            pltpu.VMEM((NI, 3 * NI), BF16),
            pltpu.VMEM((3 * NI, span + NRHS), BF16),
            pltpu.VMEM((2 * span, NI), BF16),
            pltpu.SMEM((PER_DEV,), jnp.int32),
            pltpu.SMEM((2 * n_sub,), jnp.int32),
        ],
        compiler_params=params(56),
        name="eliminate",
    )(near, owner, live, interior_inverse, coupling, interior_grad)


def couple_kernel(
    n_region, n_sub, list_ref, owner_ref, live_ref, coupling_ref, solved_ref, *rest
):
    chunks, (pay_ref, turned_ref, right_ref, slot_ref, count_ref) = rest[:8], rest[8:]
    i = pl.program_id(0)

    @pl.when(i == 0)
    def _():
        send_slots(list_ref, owner_ref, slot_ref, count_ref, n_region, n_sub)

    live = live_ref[(lax.axis_index("region") * n_sub + lax.axis_index("sub")) * SUB_DEV + i]
    for j in range(SLOTS):
        rows = slice(j * TILE, (j + 1) * TILE)
        th, tl = halves((coupling_ref[0, j] * (j < live).astype(F32)).T)
        turned_ref[rows, :NI] = th
        turned_ref[rows, NI : 2 * NI] = tl
        turned_ref[rows, 2 * NI :] = th
    right_ref[:NI] = solved_ref[0, NI:]
    right_ref[NI : 2 * NI] = solved_ref[0, :NI]
    right_ref[2 * NI :] = solved_ref[0, :NI]
    schur = product(turned_ref[...], right_ref[...])
    for j in range(SLOTS):
        slot = slot_ref[i * SLOTS + j]
        for k in range(1, SLOTS):
            other = (j + k) % SLOTS
            pay_ref[slot, :, (k - 1) * TILE : k * TILE] = schur[
                j * TILE : (j + 1) * TILE, other * TILE : (other + 1) * TILE
            ]

    @pl.when(i == SUB_DEV - 1)
    def _():
        for c in range(8):
            chunks[c][...] = pay_ref[2 * c : 2 * c + 2]


def couple(near, owner, live, coupling, solved, n_region, n_sub):
    span = SLOTS * TILE
    wide = (SLOTS - 1) * TILE
    return pl.pallas_call(
        lambda *refs: couple_kernel(n_region, n_sub, *refs),
        grid=(SUB_DEV,),
        out_shape=(jax.ShapeDtypeStruct((2, TILE, wide), F32),) * 8,
        in_specs=[SMEM] * 3
        + [
            pl.BlockSpec((1, SLOTS, NI, TILE), lambda i: (i, 0, 0, 0)),
            pl.BlockSpec((1, 2 * NI, span), lambda i: (i, 0, 0)),
        ],
        out_specs=(pl.BlockSpec((2, TILE, wide), lambda i: (0, 0, 0)),) * 8,
        scratch_shapes=[
            pltpu.VMEM((PER_DEV, TILE, wide), F32),
            pltpu.VMEM((span, 3 * NI), BF16),
            pltpu.VMEM((3 * NI, span), BF16),
            pltpu.SMEM((PER_DEV,), jnp.int32),
            pltpu.SMEM((2 * n_sub,), jnp.int32),
        ],
        compiler_params=params(32),
        cost_estimate=pl.CostEstimate(flops=8 * 10**9, bytes_accessed=12 * MIB, transcendentals=0),
        name="couple",
    )(near, owner, live, coupling, solved)


def lane_group(shape, axis):
    return lax.broadcasted_iota(jnp.int32, shape, axis) // BLOCK


def block_diagonal(w, kb):
    groups = TILE // BLOCK
    parts = []
    for m in range(groups):
        rows = w[m * BLOCK : (m + 1) * BLOCK]
        shift = ((m - kb) % groups) * BLOCK
        if shift:
            rows = pltpu.roll(rows, shift, 1)
        parts.append(jnp.where(lane_group(rows.shape, 1) == m, rows, 0.0))
    return parts


def packed_inverse(p):
    lane = lax.broadcasted_iota(jnp.int32, p.shape, 1)
    row_id = lax.broadcasted_iota(jnp.int32, p.shape, 0)
    group_base = lane // BLOCK * BLOCK
    for k in range(0, BLOCK, 2):
        first = jnp.take_along_axis(p, group_base + k, axis=1)
        second = jnp.take_along_axis(p, group_base + (k + 1), axis=1)
        a, c = first[k : k + 1], first[k + 1 : k + 2]
        b, d = second[k : k + 1], second[k + 1 : k + 2]
        recip = 1.0 / (a * d - b * c)
        at_first = lane == group_base + k
        at_second = lane == group_base + (k + 1)
        row0 = jnp.where(at_first[:1], 1.0, jnp.where(at_second[:1], 0.0, p[k : k + 1]))
        row1 = jnp.where(at_first[:1], 0.0, jnp.where(at_second[:1], 1.0, p[k + 1 : k + 2]))
        new0 = (d * row0 - b * row1) * recip
        new1 = (a * row1 - c * row0) * recip
        p = jnp.where(at_first | at_second, 0.0, p) - first * new0 - second * new1
        p = jnp.where(row_id == k, new0, jnp.where(row_id == k + 1, new1, p))
    return p


def batch_inverse(tiles):
    groups = TILE // BLOCK
    w = [
        jnp.concatenate([t[kb * BLOCK : (kb + 1) * BLOCK] for t in tiles], axis=0) for kb in range(groups)
    ]
    lane = lax.broadcasted_iota(jnp.int32, (TILE, TILE), 1)
    row_in = lax.broadcasted_iota(jnp.int32, (TILE, TILE), 0) % BLOCK
    for kb in range(groups):
        parts = block_diagonal(w[kb], kb)
        packed = packed_inverse(parts[0] + parts[1] + parts[2] + parts[3])
        inner = jnp.concatenate(
            [jnp.where(lane_group(packed.shape, 1) == m, packed, 0.0) for m in range(groups)], axis=0
        )
        in_block = lane // BLOCK == kb
        unit = (lane == kb * BLOCK + row_in).astype(F32)
        pivot = dot3(halves(inner), halves(jnp.where(in_block, unit, w[kb])))
        pivot_parts = halves(pivot)
        for other in range(groups):
            if other == kb:
                continue
            left = jnp.concatenate(block_diagonal(w[other], kb), axis=0)
            w[other] = jnp.where(in_block, 0.0, w[other]) - dot3(halves(left), pivot_parts)
        w[kb] = pivot
    return [
        jnp.concatenate([w[kb][m * BLOCK : (m + 1) * BLOCK] for kb in range(groups)], axis=0)
        for m in range(SEP_DEV)
    ]


def folded(x):
    return jnp.sum(x.reshape(-1, 8, x.shape[-1]), axis=0)


def gather_kernel(target_ref, next_ref, c0, c1, c2, c3, here_ref, next_sum_ref):
    here_ref[...] = jnp.zeros(here_ref.shape, F32)
    next_sum_ref[...] = jnp.zeros(here_ref.shape, F32)
    for turn, chunk in enumerate((c0, c1, c2, c3)):
        for rank in range(2):
            t = target_ref[2 * turn + rank]
            here_ref[t] = here_ref[t] + chunk[rank]
            t = next_ref[2 * turn + rank]
            next_sum_ref[t] = next_sum_ref[t] + chunk[2 + rank]


def gather(target, later, chunks):
    total = jax.ShapeDtypeStruct((SEP_DEV, PACKED + TILE, TILE), F32)
    return pl.pallas_call(
        gather_kernel,
        out_shape=(total, total),
        in_specs=[SMEM] * 2 + [VMEM] * 4,
        out_specs=(VMEM,) * 2,
        compiler_params=params(8),
        name="gather",
    )(target, later, *chunks)


def invert_kernel(hess_ref, grad_ref, here_ref, got_ref, inv_ref, u_ref):
    tiles = []
    for t in range(SEP_DEV):
        total = here_ref[t] + got_ref[t]
        tiles.append(hess_ref[t] - unpack_symmetric(total[:PACKED]))
        u_ref[t] = grad_ref[t] - total[PACKED:]
    inverses = batch_inverse(tiles)
    for t in range(SEP_DEV):
        inv_ref[t] = stack_halves(inverses[t])


def invert(hess, grad, here, got):
    return pl.pallas_call(
        invert_kernel,
        out_shape=(
            jax.ShapeDtypeStruct((SEP_DEV, 2 * TILE, TILE), BF16),
            jax.ShapeDtypeStruct((SEP_DEV, TILE, NRHS), F32),
        ),
        in_specs=[VMEM] * 4,
        out_specs=(VMEM,) * 2,
        compiler_params=params(14),
        cost_estimate=pl.CostEstimate(flops=10**10, bytes_accessed=4 * MIB, transcendentals=0),
        name="invert",
    )(hess, grad, here, got)


def precondition(inv_ref, u_ref, earlier, w_ref):
    norm = jnp.zeros((8, NRHS), F32)
    for t in range(SEP_DEV):
        u = u_ref[t]
        w = dot4(inv_ref[t], pair_halves(u))
        w_ref[t * TILE : (t + 1) * TILE] = w
        norm = norm + folded(u * w)
    norm = jnp.sum(norm, axis=0, keepdims=True)
    row = lax.broadcasted_iota(jnp.int32, (NORM_ROWS, NRHS), 0)
    w_ref[SEP_DEV * TILE :] = jnp.where(row == 0, norm if earlier is None else earlier, jnp.where(row == 1, norm, 0.0))


WIDE = jax.ShapeDtypeStruct((SPREAD, NRHS), F32)


def begin(inv, u):
    return pl.pallas_call(
        lambda inv_ref, u_ref, w_ref: precondition(inv_ref, u_ref, None, w_ref),
        out_shape=WIDE,
        in_specs=[VMEM] * 2,
        out_specs=VMEM,
        compiler_params=params(8),
        name="begin",
    )(inv, u)


def lay_out(pieces, v_ref, sides):
    for piece, spots in zip(pieces, PIECES):
        for n, (side, turn) in enumerate(spots):
            if side not in sides:
                continue
            for t in range(SEP_DEV):
                where = (sides.index(side) * 4 + turn) * SEP_DEV + t
                rows = n * SPREAD + t * TILE
                v_ref[where] = pair_halves(piece[rows : rows + TILE])


def scatter(target_ref, seen_ref, offs, v_ref, u_ref):
    u_ref[...] = jnp.zeros(u_ref.shape, F32)
    for a in range(PER_DEV):
        t = target_ref[a]
        right = [v_ref[seen_ref[a * (SLOTS - 1) + k]] for k in range(SLOTS - 1)]
        off = offs[a // 2][a % 2] if a < 10 else offs[5][a - 10]
        u_ref[t] = u_ref[t] + dot4(stack_halves(off), jnp.concatenate(right, axis=0))


def apply_kernel(target_ref, seen_ref, inv_ref, *rest):
    offs, pieces, (u_ref, w_ref, v_ref) = rest[:6], rest[6:14], rest[14:]
    lay_out(pieces, v_ref, (0, 1, 2))
    scatter(target_ref, seen_ref, offs, v_ref, u_ref)
    precondition(inv_ref, u_ref, pieces[0][SEP_DEV * TILE : SEP_DEV * TILE + 1], w_ref)


def apply(target, seen, inv, offs, pieces):
    tile = jax.ShapeDtypeStruct((SEP_DEV, TILE, NRHS), F32)
    return pl.pallas_call(
        apply_kernel,
        out_shape=(tile, WIDE),
        in_specs=[SMEM] * 2 + [VMEM] * 15,
        out_specs=(VMEM,) * 2,
        scratch_shapes=[pltpu.VMEM((12 * SEP_DEV, TILE, 2 * NRHS), BF16)],
        compiler_params=params(16),
        cost_estimate=pl.CostEstimate(flops=2 * 10**9, bytes_accessed=7 * MIB, transcendentals=0),
        name="apply",
    )(target, seen, inv, *offs, *pieces)


def listed(own_ref, v_ref, i):
    tiles = []
    for j in range(SLOTS):
        n = own_ref[i * SLOTS + j]
        tiles.append(v_ref[n])
    return jnp.concatenate(tiles, axis=0)


def ahead_kernel(own_ref, solved_ref, *rest):
    first, second, (ya_ref, yb_ref, v_ref) = rest[:8], rest[8:16], rest[16:]
    for pieces, y_ref in ((first, ya_ref), (second, yb_ref)):
        lay_out(pieces, v_ref, (0, 1, 2))
        for i in range(SUB_DEV):
            y_ref[i] = dot4(solved_ref[i], listed(own_ref, v_ref, i))


def ahead(own, solved, w0s, w1s):
    y = jax.ShapeDtypeStruct((SUB_DEV, NI, NRHS), F32)
    return pl.pallas_call(
        ahead_kernel,
        out_shape=(y, y),
        in_specs=[SMEM] + [VMEM] * 17,
        out_specs=(VMEM,) * 2,
        scratch_shapes=[pltpu.VMEM((12 * SEP_DEV, TILE, 2 * NRHS), BF16)],
        compiler_params=params(28),
        cost_estimate=pl.CostEstimate(flops=8 * 10**9, bytes_accessed=14 * MIB, transcendentals=0),
        name="ahead",
    )(own, solved, *w0s, *w1s)


def finish_kernel(
    target_ref, seen_ref, own_ref, norm_ref, solved_ref, reduced_ref, ya_ref, yb_ref, u1_ref, w0_ref, w1_ref, *rest
):
    offs, pieces, (interior_ref, x_ref, resid_ref, v_ref, u_ref) = rest[:6], rest[6:14], rest[14:]
    whole = lambda x: jnp.sum(jnp.sum(x, axis=0, keepdims=True), axis=1, keepdims=True)
    q = whole(norm_ref[1:2]) / whole(norm_ref[:1])
    g1 = 1.0 / (2.0 - q)
    g2 = 1.0 / (2.0 - q * g1)
    back = q * g2 * g1
    c0 = 1.0 + (1.0 + back) * g1 * q - 2.0 * g2 * g1 * q
    c1 = (1.0 + back) * g1 * 2.0
    c2 = 4.0 * g2 * g1
    lay_out(pieces, v_ref, (0, 1, 2))
    for i in range(SUB_DEV):
        y = dot4(solved_ref[i], listed(own_ref, v_ref, i))
        interior_ref[i] = reduced_ref[i] - (c0 * ya_ref[i] + c1 * yb_ref[i] + c2 * y)
    scatter(target_ref, seen_ref, offs, v_ref, u_ref)
    for t in range(SEP_DEV):
        rows = slice(t * TILE, (t + 1) * TILE)
        x_ref[t] = c0 * w0_ref[rows] + c1 * w1_ref[rows] + c2 * pieces[0][rows]
        resid_ref[t] = g1 * g2 * (4.0 * u_ref[t] - 3.0 * q * u1_ref[t])


def finish(target, seen, own, norms, solved, reduced, ya, yb, u1, w0, w1, offs, w2s):
    tile = jax.ShapeDtypeStruct((SEP_DEV, TILE, NRHS), F32)
    return pl.pallas_call(
        finish_kernel,
        out_shape=(jax.ShapeDtypeStruct((SUB_DEV, NI, NRHS), F32), tile, tile),
        in_specs=[SMEM] * 3 + [VMEM] * 22,
        out_specs=(VMEM,) * 3,
        scratch_shapes=[
            pltpu.VMEM((12 * SEP_DEV, TILE, 2 * NRHS), BF16),
            pltpu.VMEM((SEP_DEV, TILE, NRHS), F32),
        ],
        compiler_params=params(30),
        name="finish",
    )(target, seen, own, norms, solved, reduced, ya, yb, u1, w0, w1, *offs, *w2s)


def per_device(
    interior_inverse, coupling, interior_grad, separator_hessian_blocks, sep_grad, lists, owner, counts
):
    n_region = lax.axis_size("region")
    n_sub = lax.axis_size("sub")
    region = lax.axis_index("region")
    both = ("region", "sub")

    def shift(x, ahead, turn):
        pairs = [
            (r * n_sub + s, (r + ahead) % n_region * n_sub + (s + turn) % n_sub)
            for r in range(n_region)
            for s in range(n_sub)
        ]
        return lax.ppermute(x, both, pairs)

    def swap(x, partner):
        pairs = [(r * n_sub + s, partner(r) * n_sub + s) for r in range(n_region) for s in range(n_sub)]
        return lax.ppermute(x, both, pairs)

    def across(x):
        return swap(x, lambda r: (r + 1 if r % 2 else r - 1) % n_region)

    def mate(x):
        return swap(x, lambda r: r ^ 1)

    def add_over(x, steps):
        for step in steps:
            x = x + swap(x, lambda r: r ^ step)
        return x

    def around(chunks):
        return [chunks[0]] + [shift(chunks[turn], 0, turn) for turn in range(1, n_sub)]

    def spread(v, small=None, steps=((), ())):
        z1, z3, z2 = (shift(v, 0, turn) for turn in (1, 3, 2))
        if small is None:
            small = sum(x[SEP_DEV * TILE :] for x in (v, z1, z3, z2))
        pair = jnp.concatenate([z1, z3], axis=0)
        pair_across = across(pair)
        if steps[0]:
            small, z2 = lax.optimization_barrier((small, z2))
            small = add_over(small, steps[0])
        z2_across = across(z2)
        all_mate = mate(jnp.concatenate([v, z1, z3, z2], axis=0))
        if steps[1]:
            small, all_mate = lax.optimization_barrier((small, all_mate))
            small = add_over(small, steps[1])
        return [v, z1, z3, z2, across(v), pair_across, z2_across, all_mate], small

    per_region = n_sub * SUB_DEV
    here = lax.dynamic_slice_in_dim(lists, region * per_region, per_region, 0)
    behind = lax.dynamic_slice_in_dim(lists, (region - 1) % n_region * per_region, per_region, 0)
    near = jnp.concatenate([behind, here], axis=0).reshape(-1)
    key = (near, owner)

    solved, reduced, *pay = eliminate(*key, counts, interior_inverse, coupling, interior_grad, n_region, n_sub)
    arrived = around(pay)
    target, seen, own, later = plan(*key, n_region, n_sub)
    offs = couple(*key, counts, coupling, solved, n_region, n_sub)
    arrived, offs = lax.optimization_barrier((arrived, offs))
    far = around(offs[4:])
    here, following = gather(target, later, arrived)
    got = shift(following, 1, 0)
    inv, u0 = invert(separator_hessian_blocks, sep_grad, here, got)
    straight = shift(far[0], 1, 0)
    u0, far[1], far[3], straight = lax.optimization_barrier((u0, far[1], far[3], straight))
    forwarded = shift(jnp.concatenate(far[1:], axis=0), 1, 0)
    w0 = begin(inv, u0)
    w0s, _ = spread(w0, u0[0, :NORM_ROWS])
    offs = around(offs[:4]) + [straight, forwarded]
    u1, w1 = apply(target, seen, inv, offs, w0s)
    w1s, norms = spread(w1, None, ((), (1, 2)))
    u2, w2 = apply(target, seen, inv, offs, w1s)
    w2s, norms = spread(w2, norms, ((4,), (8, 16)))
    ya, yb = ahead(own, solved, w0s, w1s)
    return finish(target, seen, own, norms, solved, reduced, ya, yb, u1, w0, w1, offs, w2s)


def solution(mesh):
    split3 = P(("region", "sub"), None, None)
    placed = (split3, P(("region", "sub"), None, None, None), split3, split3, split3, P(), P(), P())
    return jax.shard_map(
        per_device, mesh=mesh, in_specs=placed, out_specs=(split3, split3, split3), check_vma=False
    )
```

```python
import jax
import jax.numpy as jnp
from jax import lax
from jax.experimental import pallas as pl
from jax.experimental.pallas import tpu as pltpu
from jax.sharding import PartitionSpec as P

F32 = jnp.float32
BF16 = jnp.bfloat16
SUB_DEV = 4
SLOTS = 4
TILE = 128
NI = 512
NRHS = 128
SEP_DEV = 4
PER_DEV = SUB_DEV * SLOTS
BLOCK = 32
MIB = 1024 * 1024

PIECES = [
    [(0, 0)], [(0, 1)], [(0, 3)], [(0, 2)],
    [(1, 0)], [(1, 1), (1, 3)], [(1, 2)],
    [(2, 0), (2, 1), (2, 3), (2, 2)],
]
HALF = TILE // 2
PACKED = HALF + 8
NORM_ROWS = 8
SPREAD = SEP_DEV * TILE + NORM_ROWS


def halves(x):
    high = x.astype(BF16)
    low = (x - high.astype(F32)).astype(BF16)
    return high, low


def product(a, b):
    return lax.dot_general(a, b, (((1,), (0,)), ((), ())), preferred_element_type=F32)


def dot3(a, b):
    (ah, al), (bh, bl) = a, b
    return product(jnp.concatenate([ah, al, ah], 1), jnp.concatenate([bl, bh, bh], 0))


def dot4(stacked, paired):
    m, n = stacked.shape[0] // 2, paired.shape[1] // 2
    r = product(stacked, paired)
    return (r[m:, n:] + (r[m:, :n] + r[:m, n:])) + r[:m, :n]


def stack_halves(x):
    return jnp.concatenate(halves(x), axis=0)


def pair_halves(x):
    return jnp.concatenate(halves(x), axis=1)


def params(mib):
    return pltpu.CompilerParams(vmem_limit_bytes=mib * MIB)


SMEM = pl.BlockSpec(memory_space=pltpu.SMEM)
VMEM = pl.BlockSpec(memory_space=pltpu.VMEM)


def log2(n):
    assert n & (n - 1) == 0
    return n.bit_length() - 1


def send_slots(list_ref, owner_ref, slot_ref, count_ref, n_region, n_sub):
    region, sub = lax.axis_index("region"), lax.axis_index("sub")
    begin = (n_sub + sub) * PER_DEV
    for c in range(2 * n_sub):
        count_ref[c] = 0

    def step(n, carry):
        dev = owner_ref[list_ref[begin + n]] >> log2(SEP_DEV)
        ahead = ((dev >> log2(n_sub)) - region) & (n_region - 1)
        turn = (dev - sub) & (n_sub - 1)
        key = ((ahead & 1) << log2(n_sub)) + turn
        rank = count_ref[key]
        count_ref[key] = rank + 1
        slot_ref[n] = key * 2 + rank
        return carry

    lax.fori_loop(0, PER_DEV, step, 0)


def plan_kernel(n_region, n_sub, list_ref, owner_ref, target_ref, seen_ref, own_ref, next_ref):
    region, sub = lax.axis_index("region"), lax.axis_index("sub")
    me = region * n_sub + sub
    after = ((region + 1) & (n_region - 1)) * n_sub + sub

    def tile_at(pos):
        dev = pos >> log2(SEP_DEV)
        there = dev >> log2(n_sub)
        side = jnp.where(there == region, 0, jnp.where(there == (region ^ 1), 2, 1))
        turn = (sub - dev) & (n_sub - 1)
        return (side * n_sub + turn) * SEP_DEV + (pos & (SEP_DEV - 1))

    def source_step(source, carry):
        behind = 1 - (source >> log2(n_sub))
        turn = (sub - source) & (n_sub - 1)
        first = (behind * n_sub + turn) * 2

        def step(n, carry):
            slot, later = carry
            at = source * PER_DEV + n
            pos = owner_ref[list_ref[at]]
            dev = pos >> log2(SEP_DEV)
            mine = dev == me
            ahead = (dev == after) & (behind == 0)

            @pl.when(mine)
            def _():
                target_ref[slot] = pos & (SEP_DEV - 1)
                base = at & ~(SLOTS - 1)
                for k in range(1, SLOTS):
                    other = owner_ref[list_ref[base + ((n + k) & (SLOTS - 1))]]
                    seen_ref[slot * (SLOTS - 1) + k - 1] = tile_at(other)

            @pl.when(ahead)
            def _():
                next_ref[later] = pos & (SEP_DEV - 1)

            return jnp.where(mine, slot + 1, slot), jnp.where(ahead, later + 1, later)

        lax.fori_loop(0, PER_DEV, step, (first, turn * 2), unroll=4)
        return carry

    lax.fori_loop(0, 2 * n_sub, source_step, 0)
    begin = (n_sub + sub) * PER_DEV

    def mine(i, carry):
        own_ref[i] = tile_at(owner_ref[list_ref[begin + i]])
        return carry

    lax.fori_loop(0, PER_DEV, mine, 0)


def plan(near, owner, n_region, n_sub):
    shapes = (PER_DEV, PER_DEV * (SLOTS - 1), PER_DEV, 2 * n_sub)
    return pl.pallas_call(
        lambda *refs: plan_kernel(n_region, n_sub, *refs),
        out_shape=tuple(jax.ShapeDtypeStruct((n,), jnp.int32) for n in shapes),
        in_specs=[SMEM] * 2,
        out_specs=(SMEM,) * 4,
        compiler_params=params(2),
        cost_estimate=pl.CostEstimate(flops=2 * 10**9, bytes_accessed=8192, transcendentals=0),
        name="plan",
    )(near, owner)


def pack_symmetric(t):
    row = lax.broadcasted_iota(jnp.int32, (HALF, TILE), 0)
    lane = lax.broadcasted_iota(jnp.int32, (HALF, TILE), 1)
    top, low = t[:HALF], t[HALF:]
    body = jnp.where(row <= lane, top, pltpu.roll(low, HALF, 1))
    ends = jnp.sum(jnp.where(row == lane - HALF, low, 0.0), axis=0, keepdims=True)
    return jnp.concatenate([body, jnp.broadcast_to(ends, (8, TILE))], axis=0)


def unpack_symmetric(f):
    row = lax.broadcasted_iota(jnp.int32, (HALF, TILE), 0)
    lane = lax.broadcasted_iota(jnp.int32, (HALF, TILE), 1)
    body, ends = f[:HALF], f[HALF : HALF + 1]
    top = jnp.where(row < lane, body, 0.0)
    low = jnp.where((row > lane - HALF) & (lane >= HALF), pltpu.roll(body, HALF, 1), 0.0)
    part = jnp.concatenate([top, low], axis=0)
    ends = jnp.where(row == lane - HALF, ends, 0.0)
    diagonal = jnp.concatenate([jnp.where(row == lane, body, 0.0), ends], axis=0)
    return part + part.T + diagonal


def eliminate_kernel(
    n_region, n_sub, list_ref, owner_ref, live_ref, inverse_ref, coupling_ref, grad_ref,
    solved_ref, reduced_ref, *rest
):
    chunks, (pay_ref, left_ref, right_ref, turned_ref, slot_ref, count_ref) = rest[:4], rest[4:]
    i = pl.program_id(0)
    span = SLOTS * TILE

    @pl.when(i == 0)
    def _():
        send_slots(list_ref, owner_ref, slot_ref, count_ref, n_region, n_sub)

    live = live_ref[(lax.axis_index("region") * n_sub + lax.axis_index("sub")) * SUB_DEV + i]
    ah, al = halves(inverse_ref[0])
    left_ref[:NI] = ah
    left_ref[NI:] = al
    for j in range(SLOTS + 1):
        x = grad_ref[0] if j == SLOTS else coupling_ref[0, j] * (j < live).astype(F32)
        cols = slice(j * TILE, (j + 1) * TILE)
        high, low = halves(x)
        right_ref[:, cols] = high
        right_ref[:, j * TILE + span + NRHS : (j + 1) * TILE + span + NRHS] = low
        if j < SLOTS:
            th, tl = halves(x.T)
            turned_ref[2 * j * TILE : (2 * j + 1) * TILE] = th
            turned_ref[(2 * j + 1) * TILE : (2 * j + 2) * TILE] = tl
    low_cols = span + NRHS
    both = (
        product(left_ref[NI:], right_ref[:, :span])
        + product(left_ref[:NI], right_ref[:, low_cols : low_cols + span])
    ) + product(left_ref[:NI], right_ref[:, :span])
    grad = jnp.concatenate([right_ref[:, span:low_cols], right_ref[:, low_cols + span :]], axis=1)
    reduced = dot4(left_ref[...], grad)
    reduced_ref[0] = reduced
    pushed = product(turned_ref[...], pair_halves(reduced))
    for j in range(SLOTS):
        cols = slice(j * TILE, (j + 1) * TILE)
        sh, sl = halves(both[:, cols])
        solved_ref[0, :NI, cols] = sh
        solved_ref[0, NI:, cols] = sl
        slot = slot_ref[i * SLOTS + j]
        diagonal = dot4(turned_ref[2 * j * TILE : (2 * j + 2) * TILE], jnp.concatenate([sh, sl], axis=1))
        pay_ref[slot, :PACKED] = pack_symmetric(diagonal)
        part = pushed[2 * j * TILE : (2 * j + 2) * TILE]
        pay_ref[slot, PACKED:] = (part[TILE:, NRHS:] + (part[TILE:, :NRHS] + part[:TILE, NRHS:])) + part[:TILE, :NRHS]

    @pl.when(i == SUB_DEV - 1)
    def _():
        for c in range(4):
            chunks[c][:2] = pay_ref[2 * c : 2 * c + 2]
            chunks[c][2:] = pay_ref[8 + 2 * c : 10 + 2 * c]


def eliminate(near, owner, live, interior_inverse, coupling, interior_grad, n_region, n_sub):
    span = SLOTS * TILE
    tall = PACKED + TILE
    step = lambda i: (i, 0, 0)
    return pl.pallas_call(
        lambda *refs: eliminate_kernel(n_region, n_sub, *refs),
        grid=(SUB_DEV,),
        out_shape=(
            jax.ShapeDtypeStruct((SUB_DEV, 2 * NI, span), BF16),
            jax.ShapeDtypeStruct((SUB_DEV, NI, NRHS), F32),
        )
        + (jax.ShapeDtypeStruct((4, tall, TILE), F32),) * 4,
        in_specs=[SMEM] * 3
        + [
            pl.BlockSpec((1, NI, NI), step),
            pl.BlockSpec((1, SLOTS, NI, TILE), lambda i: (i, 0, 0, 0)),
            pl.BlockSpec((1, NI, NRHS), step),
        ],
        out_specs=(pl.BlockSpec((1, 2 * NI, span), step), pl.BlockSpec((1, NI, NRHS), step))
        + (pl.BlockSpec((4, tall, TILE), lambda i: (0, 0, 0)),) * 4,
        scratch_shapes=[
            pltpu.VMEM((PER_DEV, tall, TILE), F32),
            pltpu.VMEM((2 * NI, NI), BF16),
            pltpu.VMEM((NI, 2 * (span + NRHS)), BF16),
            pltpu.VMEM((2 * span, NI), BF16),
            pltpu.SMEM((PER_DEV,), jnp.int32),
            pltpu.SMEM((2 * n_sub,), jnp.int32),
        ],
        compiler_params=params(56),
        name="eliminate",
    )(near, owner, live, interior_inverse, coupling, interior_grad)


def couple_kernel(
    n_region, n_sub, list_ref, owner_ref, live_ref, coupling_ref, solved_ref, *rest
):
    chunks, (pay_ref, turned_ref, right_ref, slot_ref, count_ref) = rest[:8], rest[8:]
    i = pl.program_id(0)

    @pl.when(i == 0)
    def _():
        send_slots(list_ref, owner_ref, slot_ref, count_ref, n_region, n_sub)

    live = live_ref[(lax.axis_index("region") * n_sub + lax.axis_index("sub")) * SUB_DEV + i]
    for j in range(SLOTS):
        rows = slice(j * TILE, (j + 1) * TILE)
        th, tl = halves((coupling_ref[0, j] * (j < live).astype(F32)).T)
        turned_ref[rows, :NI] = th
        turned_ref[rows, NI : 2 * NI] = tl
        turned_ref[rows, 2 * NI :] = th
    right_ref[:NI] = solved_ref[0, NI:]
    right_ref[NI : 2 * NI] = solved_ref[0, :NI]
    right_ref[2 * NI :] = solved_ref[0, :NI]
    schur = product(turned_ref[...], right_ref[...])
    for j in range(SLOTS):
        slot = slot_ref[i * SLOTS + j]
        for k in range(1, SLOTS):
            other = (j + k) % SLOTS
            pay_ref[slot, :, (k - 1) * TILE : k * TILE] = schur[
                j * TILE : (j + 1) * TILE, other * TILE : (other + 1) * TILE
            ]

    @pl.when(i == SUB_DEV - 1)
    def _():
        for c in range(8):
            chunks[c][...] = pay_ref[2 * c : 2 * c + 2]


def couple(near, owner, live, coupling, solved, n_region, n_sub):
    span = SLOTS * TILE
    wide = (SLOTS - 1) * TILE
    return pl.pallas_call(
        lambda *refs: couple_kernel(n_region, n_sub, *refs),
        grid=(SUB_DEV,),
        out_shape=(jax.ShapeDtypeStruct((2, TILE, wide), F32),) * 8,
        in_specs=[SMEM] * 3
        + [
            pl.BlockSpec((1, SLOTS, NI, TILE), lambda i: (i, 0, 0, 0)),
            pl.BlockSpec((1, 2 * NI, span), lambda i: (i, 0, 0)),
        ],
        out_specs=(pl.BlockSpec((2, TILE, wide), lambda i: (0, 0, 0)),) * 8,
        scratch_shapes=[
            pltpu.VMEM((PER_DEV, TILE, wide), F32),
            pltpu.VMEM((span, 3 * NI), BF16),
            pltpu.VMEM((3 * NI, span), BF16),
            pltpu.SMEM((PER_DEV,), jnp.int32),
            pltpu.SMEM((2 * n_sub,), jnp.int32),
        ],
        compiler_params=params(32),
        cost_estimate=pl.CostEstimate(flops=8 * 10**9, bytes_accessed=12 * MIB, transcendentals=0),
        name="couple",
    )(near, owner, live, coupling, solved)


def lane_group(shape, axis):
    return lax.broadcasted_iota(jnp.int32, shape, axis) // BLOCK


def block_diagonal(w, kb):
    groups = TILE // BLOCK
    parts = []
    for m in range(groups):
        rows = w[m * BLOCK : (m + 1) * BLOCK]
        shift = ((m - kb) % groups) * BLOCK
        if shift:
            rows = pltpu.roll(rows, shift, 1)
        parts.append(jnp.where(lane_group(rows.shape, 1) == m, rows, 0.0))
    return parts


def packed_inverse(p):
    lane = lax.broadcasted_iota(jnp.int32, p.shape, 1)
    row_id = lax.broadcasted_iota(jnp.int32, p.shape, 0)
    group_base = lane // BLOCK * BLOCK
    for k in range(0, BLOCK, 2):
        first = jnp.take_along_axis(p, group_base + k, axis=1)
        second = jnp.take_along_axis(p, group_base + (k + 1), axis=1)
        a, c = first[k : k + 1], first[k + 1 : k + 2]
        b, d = second[k : k + 1], second[k + 1 : k + 2]
        recip = 1.0 / (a * d - b * c)
        at_first = lane == group_base + k
        at_second = lane == group_base + (k + 1)
        row0 = jnp.where(at_first[:1], 1.0, jnp.where(at_second[:1], 0.0, p[k : k + 1]))
        row1 = jnp.where(at_first[:1], 0.0, jnp.where(at_second[:1], 1.0, p[k + 1 : k + 2]))
        new0 = (d * row0 - b * row1) * recip
        new1 = (a * row1 - c * row0) * recip
        p = jnp.where(at_first | at_second, 0.0, p) - first * new0 - second * new1
        p = jnp.where(row_id == k, new0, jnp.where(row_id == k + 1, new1, p))
    return p


def batch_inverse(tiles):
    groups = TILE // BLOCK
    w = [
        jnp.concatenate([t[kb * BLOCK : (kb + 1) * BLOCK] for t in tiles], axis=0) for kb in range(groups)
    ]
    lane = lax.broadcasted_iota(jnp.int32, (TILE, TILE), 1)
    row_in = lax.broadcasted_iota(jnp.int32, (TILE, TILE), 0) % BLOCK
    for kb in range(groups):
        parts = block_diagonal(w[kb], kb)
        packed = packed_inverse(parts[0] + parts[1] + parts[2] + parts[3])
        inner = jnp.concatenate(
            [jnp.where(lane_group(packed.shape, 1) == m, packed, 0.0) for m in range(groups)], axis=0
        )
        in_block = lane // BLOCK == kb
        unit = (lane == kb * BLOCK + row_in).astype(F32)
        pivot = dot3(halves(inner), halves(jnp.where(in_block, unit, w[kb])))
        pivot_parts = halves(pivot)
        for other in range(groups):
            if other == kb:
                continue
            left = jnp.concatenate(block_diagonal(w[other], kb), axis=0)
            w[other] = jnp.where(in_block, 0.0, w[other]) - dot3(halves(left), pivot_parts)
        w[kb] = pivot
    return [
        jnp.concatenate([w[kb][m * BLOCK : (m + 1) * BLOCK] for kb in range(groups)], axis=0)
        for m in range(SEP_DEV)
    ]


def folded(x):
    return jnp.sum(x.reshape(-1, 8, x.shape[-1]), axis=0)


def gather_kernel(target_ref, next_ref, c0, c1, c2, c3, here_ref, next_sum_ref):
    here_ref[...] = jnp.zeros(here_ref.shape, F32)
    next_sum_ref[...] = jnp.zeros(here_ref.shape, F32)
    for turn, chunk in enumerate((c0, c1, c2, c3)):
        for rank in range(2):
            t = target_ref[2 * turn + rank]
            here_ref[t] = here_ref[t] + chunk[rank]
            t = next_ref[2 * turn + rank]
            next_sum_ref[t] = next_sum_ref[t] + chunk[2 + rank]


def gather(target, later, chunks):
    total = jax.ShapeDtypeStruct((SEP_DEV, PACKED + TILE, TILE), F32)
    return pl.pallas_call(
        gather_kernel,
        out_shape=(total, total),
        in_specs=[SMEM] * 2 + [VMEM] * 4,
        out_specs=(VMEM,) * 2,
        compiler_params=params(8),
        name="gather",
    )(target, later, *chunks)


def invert_kernel(hess_ref, grad_ref, here_ref, got_ref, inv_ref, u_ref):
    tiles = []
    for t in range(SEP_DEV):
        total = here_ref[t] + got_ref[t]
        tiles.append(hess_ref[t] - unpack_symmetric(total[:PACKED]))
        u_ref[t] = grad_ref[t] - total[PACKED:]
    inverses = batch_inverse(tiles)
    for t in range(SEP_DEV):
        inv_ref[t] = stack_halves(inverses[t])


def invert(hess, grad, here, got):
    return pl.pallas_call(
        invert_kernel,
        out_shape=(
            jax.ShapeDtypeStruct((SEP_DEV, 2 * TILE, TILE), BF16),
            jax.ShapeDtypeStruct((SEP_DEV, TILE, NRHS), F32),
        ),
        in_specs=[VMEM] * 4,
        out_specs=(VMEM,) * 2,
        compiler_params=params(14),
        cost_estimate=pl.CostEstimate(flops=10**10, bytes_accessed=4 * MIB, transcendentals=0),
        name="invert",
    )(hess, grad, here, got)


def precondition(inv_ref, u_ref, earlier, w_ref):
    norm = jnp.zeros((8, NRHS), F32)
    for t in range(SEP_DEV):
        u = u_ref[t]
        w = dot4(inv_ref[t], pair_halves(u))
        w_ref[t * TILE : (t + 1) * TILE] = w
        norm = norm + folded(u * w)
    norm = jnp.sum(norm, axis=0, keepdims=True)
    row = lax.broadcasted_iota(jnp.int32, (NORM_ROWS, NRHS), 0)
    w_ref[SEP_DEV * TILE :] = jnp.where(row == 0, norm if earlier is None else earlier, jnp.where(row == 1, norm, 0.0))


WIDE = jax.ShapeDtypeStruct((SPREAD, NRHS), F32)


def begin(inv, u):
    return pl.pallas_call(
        lambda inv_ref, u_ref, w_ref: precondition(inv_ref, u_ref, None, w_ref),
        out_shape=WIDE,
        in_specs=[VMEM] * 2,
        out_specs=VMEM,
        compiler_params=params(8),
        name="begin",
    )(inv, u)


def lay_out(pieces, v_ref, sides):
    for piece, spots in zip(pieces, PIECES):
        for n, (side, turn) in enumerate(spots):
            if side not in sides:
                continue
            for t in range(SEP_DEV):
                where = (sides.index(side) * 4 + turn) * SEP_DEV + t
                rows = n * SPREAD + t * TILE
                v_ref[where] = pair_halves(piece[rows : rows + TILE])


def scatter(target_ref, seen_ref, offs, v_ref, u_ref):
    u_ref[...] = jnp.zeros(u_ref.shape, F32)
    for a in range(PER_DEV):
        t = target_ref[a]
        right = [v_ref[seen_ref[a * (SLOTS - 1) + k]] for k in range(SLOTS - 1)]
        off = offs[a // 2][a % 2] if a < 10 else offs[5][a - 10]
        u_ref[t] = u_ref[t] + dot4(stack_halves(off), jnp.concatenate(right, axis=0))


def apply_kernel(target_ref, seen_ref, inv_ref, *rest):
    offs, pieces, (u_ref, w_ref, v_ref) = rest[:6], rest[6:14], rest[14:]
    lay_out(pieces, v_ref, (0, 1, 2))
    scatter(target_ref, seen_ref, offs, v_ref, u_ref)
    precondition(inv_ref, u_ref, pieces[0][SEP_DEV * TILE : SEP_DEV * TILE + 1], w_ref)


def apply(target, seen, inv, offs, pieces):
    tile = jax.ShapeDtypeStruct((SEP_DEV, TILE, NRHS), F32)
    return pl.pallas_call(
        apply_kernel,
        out_shape=(tile, WIDE),
        in_specs=[SMEM] * 2 + [VMEM] * 15,
        out_specs=(VMEM,) * 2,
        scratch_shapes=[pltpu.VMEM((12 * SEP_DEV, TILE, 2 * NRHS), BF16)],
        compiler_params=params(16),
        cost_estimate=pl.CostEstimate(flops=2 * 10**9, bytes_accessed=7 * MIB, transcendentals=0),
        name="apply",
    )(target, seen, inv, *offs, *pieces)


def listed(own_ref, v_ref, i):
    tiles = []
    for j in range(SLOTS):
        n = own_ref[i * SLOTS + j]
        tiles.append(v_ref[n])
    return jnp.concatenate(tiles, axis=0)


def ahead_kernel(own_ref, solved_ref, *rest):
    first, second, (ya_ref, yb_ref, v_ref) = rest[:8], rest[8:16], rest[16:]
    for pieces, y_ref in ((first, ya_ref), (second, yb_ref)):
        lay_out(pieces, v_ref, (0, 1, 2))
        for i in range(SUB_DEV):
            y_ref[i] = dot4(solved_ref[i], listed(own_ref, v_ref, i))


def ahead(own, solved, w0s, w1s):
    y = jax.ShapeDtypeStruct((SUB_DEV, NI, NRHS), F32)
    return pl.pallas_call(
        ahead_kernel,
        out_shape=(y, y),
        in_specs=[SMEM] + [VMEM] * 17,
        out_specs=(VMEM,) * 2,
        scratch_shapes=[pltpu.VMEM((12 * SEP_DEV, TILE, 2 * NRHS), BF16)],
        compiler_params=params(28),
        cost_estimate=pl.CostEstimate(flops=8 * 10**9, bytes_accessed=14 * MIB, transcendentals=0),
        name="ahead",
    )(own, solved, *w0s, *w1s)


def finish_kernel(
    target_ref, seen_ref, own_ref, norm_ref, solved_ref, reduced_ref, ya_ref, yb_ref, u1_ref, w0_ref, w1_ref, *rest
):
    offs, pieces, (interior_ref, x_ref, resid_ref, v_ref, u_ref) = rest[:6], rest[6:14], rest[14:]
    whole = lambda x: jnp.sum(jnp.sum(x, axis=0, keepdims=True), axis=1, keepdims=True)
    q = whole(norm_ref[1:2]) / whole(norm_ref[:1])
    g1 = 1.0 / (2.0 - q)
    g2 = 1.0 / (2.0 - q * g1)
    back = q * g2 * g1
    c0 = 1.0 + (1.0 + back) * g1 * q - 2.0 * g2 * g1 * q
    c1 = (1.0 + back) * g1 * 2.0
    c2 = 4.0 * g2 * g1
    lay_out(pieces, v_ref, (0, 1, 2))
    for i in range(SUB_DEV):
        y = dot4(solved_ref[i], listed(own_ref, v_ref, i))
        interior_ref[i] = reduced_ref[i] - (c0 * ya_ref[i] + c1 * yb_ref[i] + c2 * y)
    scatter(target_ref, seen_ref, offs, v_ref, u_ref)
    for t in range(SEP_DEV):
        rows = slice(t * TILE, (t + 1) * TILE)
        x_ref[t] = c0 * w0_ref[rows] + c1 * w1_ref[rows] + c2 * pieces[0][rows]
        resid_ref[t] = g1 * g2 * (4.0 * u_ref[t] - 3.0 * q * u1_ref[t])


def finish(target, seen, own, norms, solved, reduced, ya, yb, u1, w0, w1, offs, w2s):
    tile = jax.ShapeDtypeStruct((SEP_DEV, TILE, NRHS), F32)
    return pl.pallas_call(
        finish_kernel,
        out_shape=(jax.ShapeDtypeStruct((SUB_DEV, NI, NRHS), F32), tile, tile),
        in_specs=[SMEM] * 3 + [VMEM] * 22,
        out_specs=(VMEM,) * 3,
        scratch_shapes=[
            pltpu.VMEM((12 * SEP_DEV, TILE, 2 * NRHS), BF16),
            pltpu.VMEM((SEP_DEV, TILE, NRHS), F32),
        ],
        compiler_params=params(30),
        name="finish",
    )(target, seen, own, norms, solved, reduced, ya, yb, u1, w0, w1, *offs, *w2s)


def per_device(
    interior_inverse, coupling, interior_grad, separator_hessian_blocks, sep_grad, lists, owner, counts
):
    n_region = lax.axis_size("region")
    n_sub = lax.axis_size("sub")
    region = lax.axis_index("region")
    both = ("region", "sub")

    def shift(x, ahead, turn):
        pairs = [
            (r * n_sub + s, (r + ahead) % n_region * n_sub + (s + turn) % n_sub)
            for r in range(n_region)
            for s in range(n_sub)
        ]
        return lax.ppermute(x, both, pairs)

    def swap(x, partner):
        pairs = [(r * n_sub + s, partner(r) * n_sub + s) for r in range(n_region) for s in range(n_sub)]
        return lax.ppermute(x, both, pairs)

    def across(x):
        return swap(x, lambda r: (r + 1 if r % 2 else r - 1) % n_region)

    def mate(x):
        return swap(x, lambda r: r ^ 1)

    def add_over(x, steps):
        for step in steps:
            x = x + swap(x, lambda r: r ^ step)
        return x

    def around(chunks):
        return [chunks[0]] + [shift(chunks[turn], 0, turn) for turn in range(1, n_sub)]

    def spread(v, small=None, steps=((), ())):
        z1, z3, z2 = (shift(v, 0, turn) for turn in (1, 3, 2))
        if small is None:
            small = sum(x[SEP_DEV * TILE :] for x in (v, z1, z3, z2))
        pair = jnp.concatenate([z1, z3], axis=0)
        pair_across = across(pair)
        if steps[0]:
            small, z2 = lax.optimization_barrier((small, z2))
            small = add_over(small, steps[0])
        z2_across = across(z2)
        all_mate = mate(jnp.concatenate([v, z1, z3, z2], axis=0))
        if steps[1]:
            small, all_mate = lax.optimization_barrier((small, all_mate))
            small = add_over(small, steps[1])
        return [v, z1, z3, z2, across(v), pair_across, z2_across, all_mate], small

    per_region = n_sub * SUB_DEV
    here = lax.dynamic_slice_in_dim(lists, region * per_region, per_region, 0)
    behind = lax.dynamic_slice_in_dim(lists, (region - 1) % n_region * per_region, per_region, 0)
    near = jnp.concatenate([behind, here], axis=0).reshape(-1)
    key = (near, owner)

    solved, reduced, *pay = eliminate(*key, counts, interior_inverse, coupling, interior_grad, n_region, n_sub)
    arrived = around(pay)
    target, seen, own, later = plan(*key, n_region, n_sub)
    offs = couple(*key, counts, coupling, solved, n_region, n_sub)
    arrived, offs = lax.optimization_barrier((arrived, offs))
    far = around(offs[4:])
    here, following = gather(target, later, arrived)
    got = shift(following, 1, 0)
    inv, u0 = invert(separator_hessian_blocks, sep_grad, here, got)
    straight = shift(far[0], 1, 0)
    u0, far[1], far[3], straight = lax.optimization_barrier((u0, far[1], far[3], straight))
    forwarded = shift(jnp.concatenate(far[1:], axis=0), 1, 0)
    w0 = begin(inv, u0)
    w0s, _ = spread(w0, u0[0, :NORM_ROWS])
    offs = around(offs[:4]) + [straight, forwarded]
    u1, w1 = apply(target, seen, inv, offs, w0s)
    w1s, norms = spread(w1, None, ((), (1, 2)))
    u2, w2 = apply(target, seen, inv, offs, w1s)
    w2s, norms = spread(w2, norms, ((4,), (8, 16)))
    ya, yb = ahead(own, solved, w0s, w1s)
    return finish(target, seen, own, norms, solved, reduced, ya, yb, u1, w0, w1, offs, w2s)


def solution(mesh):
    split3 = P(("region", "sub"), None, None)
    placed = (split3, P(("region", "sub"), None, None, None), split3, split3, split3, P(), P(), P())
    return jax.shard_map(
        per_device, mesh=mesh, in_specs=placed, out_specs=(split3, split3, split3), check_vma=False
    )
```

```python
import jax
import jax.numpy as jnp
from jax import lax
from jax.experimental import pallas as pl
from jax.experimental.pallas import tpu as pltpu
from jax.sharding import PartitionSpec as P

F32 = jnp.float32
BF16 = jnp.bfloat16
SUB_DEV = 4
SLOTS = 4
TILE = 128
NI = 512
NRHS = 128
SEP_DEV = 4
PER_DEV = SUB_DEV * SLOTS
BLOCK = 32
MIB = 1024 * 1024

PIECES = [
    [(0, 0)], [(0, 1)], [(0, 3)], [(0, 2)],
    [(1, 0)], [(1, 1), (1, 3)], [(1, 2)],
    [(2, 0), (2, 1), (2, 3), (2, 2)],
]
HALF = TILE // 2
PACKED = HALF + 8
NORM_ROWS = 8
SPREAD = SEP_DEV * TILE + NORM_ROWS


def halves(x):
    high = x.astype(BF16)
    low = (x - high.astype(F32)).astype(BF16)
    return high, low


def product(a, b):
    return lax.dot_general(a, b, (((1,), (0,)), ((), ())), preferred_element_type=F32)


def dot3(a, b):
    (ah, al), (bh, bl) = a, b
    return product(jnp.concatenate([ah, al, ah], 1), jnp.concatenate([bl, bh, bh], 0))


def dot4(stacked, paired):
    m, n = stacked.shape[0] // 2, paired.shape[1] // 2
    r = product(stacked, paired)
    return (r[m:, n:] + (r[m:, :n] + r[:m, n:])) + r[:m, :n]


def stack_halves(x):
    return jnp.concatenate(halves(x), axis=0)


def pair_halves(x):
    return jnp.concatenate(halves(x), axis=1)


def params(mib):
    return pltpu.CompilerParams(vmem_limit_bytes=mib * MIB)


SMEM = pl.BlockSpec(memory_space=pltpu.SMEM)
VMEM = pl.BlockSpec(memory_space=pltpu.VMEM)


def log2(n):
    assert n & (n - 1) == 0
    return n.bit_length() - 1


def send_slots(list_ref, owner_ref, slot_ref, count_ref, n_region, n_sub):
    region, sub = lax.axis_index("region"), lax.axis_index("sub")
    begin = (n_sub + sub) * PER_DEV
    for c in range(2 * n_sub):
        count_ref[c] = 0

    def step(n, carry):
        dev = owner_ref[list_ref[begin + n]] >> log2(SEP_DEV)
        ahead = ((dev >> log2(n_sub)) - region) & (n_region - 1)
        turn = (dev - sub) & (n_sub - 1)
        key = ((ahead & 1) << log2(n_sub)) + turn
        rank = count_ref[key]
        count_ref[key] = rank + 1
        slot_ref[n] = key * 2 + rank
        return carry

    lax.fori_loop(0, PER_DEV, step, 0)


def plan_kernel(n_region, n_sub, list_ref, owner_ref, target_ref, seen_ref, own_ref, next_ref):
    region, sub = lax.axis_index("region"), lax.axis_index("sub")
    me = region * n_sub + sub
    after = ((region + 1) & (n_region - 1)) * n_sub + sub

    def tile_at(pos):
        dev = pos >> log2(SEP_DEV)
        there = dev >> log2(n_sub)
        side = jnp.where(there == region, 0, jnp.where(there == (region ^ 1), 2, 1))
        turn = (sub - dev) & (n_sub - 1)
        return (side * n_sub + turn) * SEP_DEV + (pos & (SEP_DEV - 1))

    def source_step(source, carry):
        behind = 1 - (source >> log2(n_sub))
        turn = (sub - source) & (n_sub - 1)
        first = (behind * n_sub + turn) * 2

        def step(n, carry):
            slot, later = carry
            at = source * PER_DEV + n
            pos = owner_ref[list_ref[at]]
            dev = pos >> log2(SEP_DEV)
            mine = dev == me
            ahead = (dev == after) & (behind == 0)

            @pl.when(mine)
            def _():
                target_ref[slot] = pos & (SEP_DEV - 1)
                base = at & ~(SLOTS - 1)
                for k in range(1, SLOTS):
                    other = owner_ref[list_ref[base + ((n + k) & (SLOTS - 1))]]
                    seen_ref[slot * (SLOTS - 1) + k - 1] = tile_at(other)

            @pl.when(ahead)
            def _():
                next_ref[later] = pos & (SEP_DEV - 1)

            return jnp.where(mine, slot + 1, slot), jnp.where(ahead, later + 1, later)

        lax.fori_loop(0, PER_DEV, step, (first, turn * 2), unroll=4)
        return carry

    lax.fori_loop(0, 2 * n_sub, source_step, 0)
    begin = (n_sub + sub) * PER_DEV

    def mine(i, carry):
        own_ref[i] = tile_at(owner_ref[list_ref[begin + i]])
        return carry

    lax.fori_loop(0, PER_DEV, mine, 0)


def plan(near, owner, n_region, n_sub):
    shapes = (PER_DEV, PER_DEV * (SLOTS - 1), PER_DEV, 2 * n_sub)
    return pl.pallas_call(
        lambda *refs: plan_kernel(n_region, n_sub, *refs),
        out_shape=tuple(jax.ShapeDtypeStruct((n,), jnp.int32) for n in shapes),
        in_specs=[SMEM] * 2,
        out_specs=(SMEM,) * 4,
        compiler_params=params(2),
        cost_estimate=pl.CostEstimate(flops=2 * 10**9, bytes_accessed=8192, transcendentals=0),
        name="plan",
    )(near, owner)


def pack_symmetric(t):
    row = lax.broadcasted_iota(jnp.int32, (HALF, TILE), 0)
    lane = lax.broadcasted_iota(jnp.int32, (HALF, TILE), 1)
    top, low = t[:HALF], t[HALF:]
    body = jnp.where(row <= lane, top, pltpu.roll(low, HALF, 1))
    ends = jnp.sum(jnp.where(row == lane - HALF, low, 0.0), axis=0, keepdims=True)
    return jnp.concatenate([body, jnp.broadcast_to(ends, (8, TILE))], axis=0)


def unpack_symmetric(f):
    row = lax.broadcasted_iota(jnp.int32, (HALF, TILE), 0)
    lane = lax.broadcasted_iota(jnp.int32, (HALF, TILE), 1)
    body, ends = f[:HALF], f[HALF : HALF + 1]
    top = jnp.where(row < lane, body, 0.0)
    low = jnp.where((row > lane - HALF) & (lane >= HALF), pltpu.roll(body, HALF, 1), 0.0)
    part = jnp.concatenate([top, low], axis=0)
    ends = jnp.where(row == lane - HALF, ends, 0.0)
    diagonal = jnp.concatenate([jnp.where(row == lane, body, 0.0), ends], axis=0)
    return part + part.T + diagonal


def eliminate_kernel(
    n_region, n_sub, list_ref, owner_ref, live_ref, inverse_ref, coupling_ref, grad_ref,
    solved_ref, reduced_ref, *rest
):
    chunks, (pay_ref, left_ref, right_ref, turned_ref, slot_ref, count_ref) = rest[:4], rest[4:]
    i = pl.program_id(0)
    span = SLOTS * TILE

    @pl.when(i == 0)
    def _():
        send_slots(list_ref, owner_ref, slot_ref, count_ref, n_region, n_sub)

    live = live_ref[(lax.axis_index("region") * n_sub + lax.axis_index("sub")) * SUB_DEV + i]
    ah, al = halves(inverse_ref[0])
    left_ref[:NI] = ah
    left_ref[NI:] = al
    for j in range(SLOTS + 1):
        x = grad_ref[0] if j == SLOTS else coupling_ref[0, j] * (j < live).astype(F32)
        cols = slice(j * TILE, (j + 1) * TILE)
        high, low = halves(x)
        right_ref[:, cols] = high
        right_ref[:, j * TILE + span + NRHS : (j + 1) * TILE + span + NRHS] = low
        if j < SLOTS:
            th, tl = halves(x.T)
            turned_ref[2 * j * TILE : (2 * j + 1) * TILE] = th
            turned_ref[(2 * j + 1) * TILE : (2 * j + 2) * TILE] = tl
    low_cols = span + NRHS
    both = (
        product(left_ref[NI:], right_ref[:, :span])
        + product(left_ref[:NI], right_ref[:, low_cols : low_cols + span])
    ) + product(left_ref[:NI], right_ref[:, :span])
    grad = jnp.concatenate([right_ref[:, span:low_cols], right_ref[:, low_cols + span :]], axis=1)
    reduced = dot4(left_ref[...], grad)
    reduced_ref[0] = reduced
    pushed = product(turned_ref[...], pair_halves(reduced))
    for j in range(SLOTS):
        cols = slice(j * TILE, (j + 1) * TILE)
        sh, sl = halves(both[:, cols])
        solved_ref[0, :NI, cols] = sh
        solved_ref[0, NI:, cols] = sl
        slot = slot_ref[i * SLOTS + j]
        diagonal = dot4(turned_ref[2 * j * TILE : (2 * j + 2) * TILE], jnp.concatenate([sh, sl], axis=1))
        pay_ref[slot, :PACKED] = pack_symmetric(diagonal)
        part = pushed[2 * j * TILE : (2 * j + 2) * TILE]
        pay_ref[slot, PACKED:] = (part[TILE:, NRHS:] + (part[TILE:, :NRHS] + part[:TILE, NRHS:])) + part[:TILE, :NRHS]

    @pl.when(i == SUB_DEV - 1)
    def _():
        for c in range(4):
            chunks[c][:2] = pay_ref[2 * c : 2 * c + 2]
            chunks[c][2:] = pay_ref[8 + 2 * c : 10 + 2 * c]


def eliminate(near, owner, live, interior_inverse, coupling, interior_grad, n_region, n_sub):
    span = SLOTS * TILE
    tall = PACKED + TILE
    step = lambda i: (i, 0, 0)
    return pl.pallas_call(
        lambda *refs: eliminate_kernel(n_region, n_sub, *refs),
        grid=(SUB_DEV,),
        out_shape=(
            jax.ShapeDtypeStruct((SUB_DEV, 2 * NI, span), BF16),
            jax.ShapeDtypeStruct((SUB_DEV, NI, NRHS), F32),
        )
        + (jax.ShapeDtypeStruct((4, tall, TILE), F32),) * 4,
        in_specs=[SMEM] * 3
        + [
            pl.BlockSpec((1, NI, NI), step),
            pl.BlockSpec((1, SLOTS, NI, TILE), lambda i: (i, 0, 0, 0)),
            pl.BlockSpec((1, NI, NRHS), step),
        ],
        out_specs=(pl.BlockSpec((1, 2 * NI, span), step), pl.BlockSpec((1, NI, NRHS), step))
        + (pl.BlockSpec((4, tall, TILE), lambda i: (0, 0, 0)),) * 4,
        scratch_shapes=[
            pltpu.VMEM((PER_DEV, tall, TILE), F32),
            pltpu.VMEM((2 * NI, NI), BF16),
            pltpu.VMEM((NI, 2 * (span + NRHS)), BF16),
            pltpu.VMEM((2 * span, NI), BF16),
            pltpu.SMEM((PER_DEV,), jnp.int32),
            pltpu.SMEM((2 * n_sub,), jnp.int32),
        ],
        compiler_params=params(56),
        name="eliminate",
    )(near, owner, live, interior_inverse, coupling, interior_grad)


def couple_kernel(
    n_region, n_sub, list_ref, owner_ref, live_ref, coupling_ref, solved_ref, *rest
):
    chunks, (pay_ref, turned_ref, right_ref, slot_ref, count_ref) = rest[:8], rest[8:]
    i = pl.program_id(0)

    @pl.when(i == 0)
    def _():
        send_slots(list_ref, owner_ref, slot_ref, count_ref, n_region, n_sub)

    live = live_ref[(lax.axis_index("region") * n_sub + lax.axis_index("sub")) * SUB_DEV + i]
    for j in range(SLOTS):
        rows = slice(j * TILE, (j + 1) * TILE)
        th, tl = halves((coupling_ref[0, j] * (j < live).astype(F32)).T)
        turned_ref[rows, :NI] = th
        turned_ref[rows, NI : 2 * NI] = tl
        turned_ref[rows, 2 * NI :] = th
    right_ref[:NI] = solved_ref[0, NI:]
    right_ref[NI : 2 * NI] = solved_ref[0, :NI]
    right_ref[2 * NI :] = solved_ref[0, :NI]
    schur = product(turned_ref[...], right_ref[...])
    for j in range(SLOTS):
        slot = slot_ref[i * SLOTS + j]
        for k in range(1, SLOTS):
            other = (j + k) % SLOTS
            pay_ref[slot, :, (k - 1) * TILE : k * TILE] = schur[
                j * TILE : (j + 1) * TILE, other * TILE : (other + 1) * TILE
            ]

    @pl.when(i == SUB_DEV - 1)
    def _():
        for c in range(8):
            chunks[c][...] = pay_ref[2 * c : 2 * c + 2]


def couple(near, owner, live, coupling, solved, n_region, n_sub):
    span = SLOTS * TILE
    wide = (SLOTS - 1) * TILE
    return pl.pallas_call(
        lambda *refs: couple_kernel(n_region, n_sub, *refs),
        grid=(SUB_DEV,),
        out_shape=(jax.ShapeDtypeStruct((2, TILE, wide), F32),) * 8,
        in_specs=[SMEM] * 3
        + [
            pl.BlockSpec((1, SLOTS, NI, TILE), lambda i: (i, 0, 0, 0)),
            pl.BlockSpec((1, 2 * NI, span), lambda i: (i, 0, 0)),
        ],
        out_specs=(pl.BlockSpec((2, TILE, wide), lambda i: (0, 0, 0)),) * 8,
        scratch_shapes=[
            pltpu.VMEM((PER_DEV, TILE, wide), F32),
            pltpu.VMEM((span, 3 * NI), BF16),
            pltpu.VMEM((3 * NI, span), BF16),
            pltpu.SMEM((PER_DEV,), jnp.int32),
            pltpu.SMEM((2 * n_sub,), jnp.int32),
        ],
        compiler_params=params(32),
        cost_estimate=pl.CostEstimate(flops=8 * 10**9, bytes_accessed=12 * MIB, transcendentals=0),
        name="couple",
    )(near, owner, live, coupling, solved)


def lane_group(shape, axis):
    return lax.broadcasted_iota(jnp.int32, shape, axis) // BLOCK


def block_diagonal(w, kb):
    groups = TILE // BLOCK
    parts = []
    for m in range(groups):
        rows = w[m * BLOCK : (m + 1) * BLOCK]
        shift = ((m - kb) % groups) * BLOCK
        if shift:
            rows = pltpu.roll(rows, shift, 1)
        parts.append(jnp.where(lane_group(rows.shape, 1) == m, rows, 0.0))
    return parts


def packed_inverse(p):
    lane = lax.broadcasted_iota(jnp.int32, p.shape, 1)
    row_id = lax.broadcasted_iota(jnp.int32, p.shape, 0)
    group_base = lane // BLOCK * BLOCK
    for k in range(0, BLOCK, 2):
        first = jnp.take_along_axis(p, group_base + k, axis=1)
        second = jnp.take_along_axis(p, group_base + (k + 1), axis=1)
        a, c = first[k : k + 1], first[k + 1 : k + 2]
        b, d = second[k : k + 1], second[k + 1 : k + 2]
        recip = 1.0 / (a * d - b * c)
        at_first = lane == group_base + k
        at_second = lane == group_base + (k + 1)
        row0 = jnp.where(at_first[:1], 1.0, jnp.where(at_second[:1], 0.0, p[k : k + 1]))
        row1 = jnp.where(at_first[:1], 0.0, jnp.where(at_second[:1], 1.0, p[k + 1 : k + 2]))
        new0 = (d * row0 - b * row1) * recip
        new1 = (a * row1 - c * row0) * recip
        p = jnp.where(at_first | at_second, 0.0, p) - first * new0 - second * new1
        p = jnp.where(row_id == k, new0, jnp.where(row_id == k + 1, new1, p))
    return p


def batch_inverse(tiles):
    groups = TILE // BLOCK
    w = [
        jnp.concatenate([t[kb * BLOCK : (kb + 1) * BLOCK] for t in tiles], axis=0) for kb in range(groups)
    ]
    lane = lax.broadcasted_iota(jnp.int32, (TILE, TILE), 1)
    row_in = lax.broadcasted_iota(jnp.int32, (TILE, TILE), 0) % BLOCK
    for kb in range(groups):
        parts = block_diagonal(w[kb], kb)
        packed = packed_inverse(parts[0] + parts[1] + parts[2] + parts[3])
        inner = jnp.concatenate(
            [jnp.where(lane_group(packed.shape, 1) == m, packed, 0.0) for m in range(groups)], axis=0
        )
        in_block = lane // BLOCK == kb
        unit = (lane == kb * BLOCK + row_in).astype(F32)
        pivot = dot3(halves(inner), halves(jnp.where(in_block, unit, w[kb])))
        pivot_parts = halves(pivot)
        for other in range(groups):
            if other == kb:
                continue
            left = jnp.concatenate(block_diagonal(w[other], kb), axis=0)
            w[other] = jnp.where(in_block, 0.0, w[other]) - dot3(halves(left), pivot_parts)
        w[kb] = pivot
    return [
        jnp.concatenate([w[kb][m * BLOCK : (m + 1) * BLOCK] for kb in range(groups)], axis=0)
        for m in range(SEP_DEV)
    ]


def folded(x):
    return jnp.sum(x.reshape(-1, 8, x.shape[-1]), axis=0)


def gather_kernel(target_ref, next_ref, c0, c1, c2, c3, here_ref, next_sum_ref):
    here_ref[...] = jnp.zeros(here_ref.shape, F32)
    next_sum_ref[...] = jnp.zeros(here_ref.shape, F32)
    for turn, chunk in enumerate((c0, c1, c2, c3)):
        for rank in range(2):
            t = target_ref[2 * turn + rank]
            here_ref[t] = here_ref[t] + chunk[rank]
            t = next_ref[2 * turn + rank]
            next_sum_ref[t] = next_sum_ref[t] + chunk[2 + rank]


def gather(target, later, chunks):
    total = jax.ShapeDtypeStruct((SEP_DEV, PACKED + TILE, TILE), F32)
    return pl.pallas_call(
        gather_kernel,
        out_shape=(total, total),
        in_specs=[SMEM] * 2 + [VMEM] * 4,
        out_specs=(VMEM,) * 2,
        compiler_params=params(8),
        name="gather",
    )(target, later, *chunks)


def invert_kernel(hess_ref, grad_ref, here_ref, got_ref, inv_ref, u_ref):
    tiles = []
    for t in range(SEP_DEV):
        total = here_ref[t] + got_ref[t]
        tiles.append(hess_ref[t] - unpack_symmetric(total[:PACKED]))
        u_ref[t] = grad_ref[t] - total[PACKED:]
    inverses = batch_inverse(tiles)
    for t in range(SEP_DEV):
        inv_ref[t] = stack_halves(inverses[t])


def invert(hess, grad, here, got):
    return pl.pallas_call(
        invert_kernel,
        out_shape=(
            jax.ShapeDtypeStruct((SEP_DEV, 2 * TILE, TILE), BF16),
            jax.ShapeDtypeStruct((SEP_DEV, TILE, NRHS), F32),
        ),
        in_specs=[VMEM] * 4,
        out_specs=(VMEM,) * 2,
        compiler_params=params(14),
        cost_estimate=pl.CostEstimate(flops=10**10, bytes_accessed=4 * MIB, transcendentals=0),
        name="invert",
    )(hess, grad, here, got)


def precondition(inv_ref, u_ref, earlier, w_ref):
    norm = jnp.zeros((8, NRHS), F32)
    for t in range(SEP_DEV):
        u = u_ref[t]
        w = dot4(inv_ref[t], pair_halves(u))
        w_ref[t * TILE : (t + 1) * TILE] = w
        norm = norm + folded(u * w)
    norm = jnp.sum(norm, axis=0, keepdims=True)
    row = lax.broadcasted_iota(jnp.int32, (NORM_ROWS, NRHS), 0)
    w_ref[SEP_DEV * TILE :] = jnp.where(row == 0, norm if earlier is None else earlier, jnp.where(row == 1, norm, 0.0))


WIDE = jax.ShapeDtypeStruct((SPREAD, NRHS), F32)


def begin(inv, u):
    return pl.pallas_call(
        lambda inv_ref, u_ref, w_ref: precondition(inv_ref, u_ref, None, w_ref),
        out_shape=WIDE,
        in_specs=[VMEM] * 2,
        out_specs=VMEM,
        compiler_params=params(8),
        name="begin",
    )(inv, u)


def lay_out(pieces, v_ref, sides):
    for piece, spots in zip(pieces, PIECES):
        for n, (side, turn) in enumerate(spots):
            if side not in sides:
                continue
            for t in range(SEP_DEV):
                where = (sides.index(side) * 4 + turn) * SEP_DEV + t
                rows = n * SPREAD + t * TILE
                v_ref[where] = pair_halves(piece[rows : rows + TILE])


def scatter(target_ref, seen_ref, offs, v_ref, u_ref):
    u_ref[...] = jnp.zeros(u_ref.shape, F32)
    for a in range(PER_DEV):
        t = target_ref[a]
        right = [v_ref[seen_ref[a * (SLOTS - 1) + k]] for k in range(SLOTS - 1)]
        off = offs[a // 2][a % 2] if a < 10 else offs[5][a - 10]
        u_ref[t] = u_ref[t] + dot4(stack_halves(off), jnp.concatenate(right, axis=0))


def apply_kernel(target_ref, seen_ref, inv_ref, *rest):
    offs, pieces, (u_ref, w_ref, v_ref) = rest[:6], rest[6:14], rest[14:]
    lay_out(pieces, v_ref, (0, 1, 2))
    scatter(target_ref, seen_ref, offs, v_ref, u_ref)
    precondition(inv_ref, u_ref, pieces[0][SEP_DEV * TILE : SEP_DEV * TILE + 1], w_ref)


def apply(target, seen, inv, offs, pieces):
    tile = jax.ShapeDtypeStruct((SEP_DEV, TILE, NRHS), F32)
    return pl.pallas_call(
        apply_kernel,
        out_shape=(tile, WIDE),
        in_specs=[SMEM] * 2 + [VMEM] * 15,
        out_specs=(VMEM,) * 2,
        scratch_shapes=[pltpu.VMEM((12 * SEP_DEV, TILE, 2 * NRHS), BF16)],
        compiler_params=params(16),
        cost_estimate=pl.CostEstimate(flops=2 * 10**9, bytes_accessed=7 * MIB, transcendentals=0),
        name="apply",
    )(target, seen, inv, *offs, *pieces)


def listed(own_ref, v_ref, i):
    tiles = []
    for j in range(SLOTS):
        n = own_ref[i * SLOTS + j]
        tiles.append(v_ref[n])
    return jnp.concatenate(tiles, axis=0)


def ahead_kernel(own_ref, solved_ref, *rest):
    first, second, (ya_ref, yb_ref, v_ref) = rest[:8], rest[8:16], rest[16:]
    for pieces, y_ref in ((first, ya_ref), (second, yb_ref)):
        lay_out(pieces, v_ref, (0, 1, 2))
        for i in range(SUB_DEV):
            y_ref[i] = dot4(solved_ref[i], listed(own_ref, v_ref, i))


def ahead(own, solved, w0s, w1s):
    y = jax.ShapeDtypeStruct((SUB_DEV, NI, NRHS), F32)
    return pl.pallas_call(
        ahead_kernel,
        out_shape=(y, y),
        in_specs=[SMEM] + [VMEM] * 17,
        out_specs=(VMEM,) * 2,
        scratch_shapes=[pltpu.VMEM((12 * SEP_DEV, TILE, 2 * NRHS), BF16)],
        compiler_params=params(28),
        cost_estimate=pl.CostEstimate(flops=8 * 10**9, bytes_accessed=14 * MIB, transcendentals=0),
        name="ahead",
    )(own, solved, *w0s, *w1s)


def finish_kernel(
    target_ref, seen_ref, own_ref, norm_ref, solved_ref, reduced_ref, ya_ref, yb_ref, u1_ref, w0_ref, w1_ref, *rest
):
    offs, pieces, (interior_ref, x_ref, resid_ref, v_ref, u_ref) = rest[:6], rest[6:14], rest[14:]
    whole = lambda x: jnp.sum(jnp.sum(x, axis=0, keepdims=True), axis=1, keepdims=True)
    q = whole(norm_ref[1:2]) / whole(norm_ref[:1])
    g1 = 1.0 / (2.0 - q)
    g2 = 1.0 / (2.0 - q * g1)
    back = q * g2 * g1
    c0 = 1.0 + (1.0 + back) * g1 * q - 2.0 * g2 * g1 * q
    c1 = (1.0 + back) * g1 * 2.0
    c2 = 4.0 * g2 * g1
    lay_out(pieces, v_ref, (0, 1, 2))
    for i in range(SUB_DEV):
        y = dot4(solved_ref[i], listed(own_ref, v_ref, i))
        interior_ref[i] = reduced_ref[i] - (c0 * ya_ref[i] + c1 * yb_ref[i] + c2 * y)
    scatter(target_ref, seen_ref, offs, v_ref, u_ref)
    for t in range(SEP_DEV):
        rows = slice(t * TILE, (t + 1) * TILE)
        x_ref[t] = c0 * w0_ref[rows] + c1 * w1_ref[rows] + c2 * pieces[0][rows]
        resid_ref[t] = g1 * g2 * (4.0 * u_ref[t] - 3.0 * q * u1_ref[t])


def finish(target, seen, own, norms, solved, reduced, ya, yb, u1, w0, w1, offs, w2s):
    tile = jax.ShapeDtypeStruct((SEP_DEV, TILE, NRHS), F32)
    return pl.pallas_call(
        finish_kernel,
        out_shape=(jax.ShapeDtypeStruct((SUB_DEV, NI, NRHS), F32), tile, tile),
        in_specs=[SMEM] * 3 + [VMEM] * 22,
        out_specs=(VMEM,) * 3,
        scratch_shapes=[
            pltpu.VMEM((12 * SEP_DEV, TILE, 2 * NRHS), BF16),
            pltpu.VMEM((SEP_DEV, TILE, NRHS), F32),
        ],
        compiler_params=params(30),
        name="finish",
    )(target, seen, own, norms, solved, reduced, ya, yb, u1, w0, w1, *offs, *w2s)


def per_device(
    interior_inverse, coupling, interior_grad, separator_hessian_blocks, sep_grad, lists, owner, counts
):
    n_region = lax.axis_size("region")
    n_sub = lax.axis_size("sub")
    region = lax.axis_index("region")
    both = ("region", "sub")

    def shift(x, ahead, turn):
        pairs = [
            (r * n_sub + s, (r + ahead) % n_region * n_sub + (s + turn) % n_sub)
            for r in range(n_region)
            for s in range(n_sub)
        ]
        return lax.ppermute(x, both, pairs)

    def swap(x, partner):
        pairs = [(r * n_sub + s, partner(r) * n_sub + s) for r in range(n_region) for s in range(n_sub)]
        return lax.ppermute(x, both, pairs)

    def across(x):
        return swap(x, lambda r: (r + 1 if r % 2 else r - 1) % n_region)

    def mate(x):
        return swap(x, lambda r: r ^ 1)

    def add_over(x, steps):
        for step in steps:
            x = x + swap(x, lambda r: r ^ step)
        return x

    def around(chunks):
        return [chunks[0]] + [shift(chunks[turn], 0, turn) for turn in range(1, n_sub)]

    def spread(v, small=None, steps=()):
        z1, z3, z2 = (shift(v, 0, turn) for turn in (1, 3, 2))
        if small is None:
            small = sum(x[SEP_DEV * TILE :] for x in (v, z1, z3, z2))
        pair = jnp.concatenate([z1, z3], axis=0)
        pair_across = across(pair)
        z2_across = across(z2)
        all_mate = mate(jnp.concatenate([v, z1, z3, z2], axis=0))
        if steps:
            small, _ = lax.optimization_barrier((small, z2))
            small = add_over(small, steps)
            small, all_mate = lax.optimization_barrier((small, all_mate))
        return [v, z1, z3, z2, across(v), pair_across, z2_across, all_mate], small

    per_region = n_sub * SUB_DEV
    here = lax.dynamic_slice_in_dim(lists, region * per_region, per_region, 0)
    behind = lax.dynamic_slice_in_dim(lists, (region - 1) % n_region * per_region, per_region, 0)
    near = jnp.concatenate([behind, here], axis=0).reshape(-1)
    key = (near, owner)

    solved, reduced, *pay = eliminate(*key, counts, interior_inverse, coupling, interior_grad, n_region, n_sub)
    arrived = around(pay)
    target, seen, own, later = plan(*key, n_region, n_sub)
    offs = couple(*key, counts, coupling, solved, n_region, n_sub)
    arrived, offs = lax.optimization_barrier((arrived, offs))
    far = around(offs[4:])
    here, following = gather(target, later, arrived)
    got = shift(following, 1, 0)
    inv, u0 = invert(separator_hessian_blocks, sep_grad, here, got)
    straight = shift(far[0], 1, 0)
    u0, far[1], far[3], straight = lax.optimization_barrier((u0, far[1], far[3], straight))
    forwarded = shift(jnp.concatenate(far[1:], axis=0), 1, 0)
    w0 = begin(inv, u0)
    w0s, _ = spread(w0, u0[0, :NORM_ROWS])
    offs = around(offs[:4]) + [straight, forwarded]
    u1, w1 = apply(target, seen, inv, offs, w0s)
    w1s, norms = spread(w1, None, (1, 2))
    u2, w2 = apply(target, seen, inv, offs, w1s)
    w2s, norms = spread(w2, norms, (4, 8, 16))
    ya, yb = ahead(own, solved, w0s, w1s)
    return finish(target, seen, own, norms, solved, reduced, ya, yb, u1, w0, w1, offs, w2s)


def solution(mesh):
    split3 = P(("region", "sub"), None, None)
    placed = (split3, P(("region", "sub"), None, None, None), split3, split3, split3, P(), P(), P())
    return jax.shard_map(
        per_device, mesh=mesh, in_specs=placed, out_specs=(split3, split3, split3), check_vma=False
    )
```
